128 devices in a mesh: dp: 32 (over y, z, core), replica: 4 (over x).
Axes of the slice: x: 4, y: 4, z: 4, core: 2. Of those that a mesh axis runs over, the one named last changes fastest.
Arguments:
- replay: bfloat16 [1024, 24, 81, 232], P(('dp', 'replica')), may hold values from -6 to 6
- instructions: bfloat16 [1024, 512], P(('dp', 'replica')), may hold values from -6 to 6
- owners: int32 [4608, 1], P(('dp', 'replica')), may hold values from 0 to 31; in each aligned block of 36 rows (0 to 35, 36 to 71, ...) at most 3 rows name the same one
- episode_rows: int32 [4608], P(('dp', 'replica')), may hold values from 0 to 7
- frame_steps: int32 [4608], P(('dp', 'replica')), may hold values from 0 to 23
- w_expand: bfloat16 [232, 1392], replicated, may hold values from -0.375 to 0.375
- dw_kernel: float32 [9, 1392], replicated, may hold values from -2 to 2
- w_project: bfloat16 [1392, 384], replicated, may hold values from -0.15625 to 0.15625
- film_weight: bfloat16 [512, 768], replicated, may hold values from -0.25 to 0.25
- token_grad: bfloat16 [768, 6, 81, 384], P(('dp', 'replica')), may hold values from -0.0390625 to 0.0390625
Outputs:
- tokens: bfloat16 [768, 6, 81, 384], P(('dp', 'replica'))
- grad_expand: float32 [232, 1392], replicated
- grad_kernel: float32 [9, 1392], replicated
- grad_project: float32 [1392, 384], replicated
- grad_film: float32 [512, 768], replicated
The draws below stay inside these ranges and needn't reach their ends.
Inputs may be any that keep to these rules, and one draw needn't show every extreme that they name: `owners`: among the 36 request rows of one device, no owner is named more than 3 times, and some device names some owner exactly 3 times.
All inputs are finite; a program needn't handle non-finite values.
Results may differ from the reference program's by a relative error of at most 0.006.
Values may be sent and summed in bfloat16 or wider, within the bound.
A program may use at most 448 MiB of HBM per device.

```python
import math
import jax
import jax.numpy as jnp
import numpy as np
from jax import lax

CIN = 232
HID = 1392
COUT = 384
EMB = 512
SIDE = 9
STEPS = 6
EP_LEN = 24
EP_DEV = 8
CELLS = 81
FR_DEV = 36
CAPF = 3
EPISODES = 1024
WINDOWS = 768
FRAMES = 4608
N_DP = 32
N_REPLICA = 4
DEVICES = 128


def set_ends(drawn, key, least, high):
    spot = [jax.random.randint(jax.random.fold_in(key, axis), (), 0, length) for axis, length in enumerate(drawn.shape)]
    main_axis = drawn.shape.index(max(drawn.shape))
    beside = spot[:main_axis] + [(spot[main_axis] + 1) % drawn.shape[main_axis]] + spot[main_axis + 1:]
    return drawn.at[tuple(spot)].set(least).at[tuple(beside)].set(high)


def level_of(rng, extent, split, low, top_value):
    level, own = 1.0, jax.random.fold_in(rng, 6)
    for dim, parts in split:
        heights = jnp.exp(jax.random.uniform(jax.random.fold_in(own, dim), (parts,), jnp.float32, low / len(split), top_value / len(split)))
        level = level * jnp.repeat(heights, extent[dim] // parts).reshape([-1 if axis == dim else 1 for axis in range(len(extent))])
    return level


def routed_block(key, own, number, rows, count, top, reach, lean):
    order = jax.random.permutation(key, count)
    crowded, ordinary = portions_of(count, rows * top, reach, lean, True), portions_of(count, rows * top, reach, lean, False)
    places = jnp.arange(count)

    def named(lengths, rotation):
        used = int((lengths > 0).sum())
        fixed = max(1, used // 4)
        passed = fixed + (places - fixed + rotation * (used - fixed)) % max(1, count - fixed)
        return jnp.zeros((count,), jnp.int32).at[order[jnp.where(places < fixed, places, passed)]].set(jnp.asarray(lengths, jnp.int32))

    lengths = jnp.where(number % 4 == 0, named(crowded, number // 4), named(ordinary, number - number // 4 - 1))
    mixed = jax.random.permutation(jax.random.fold_in(own, 3), count)
    donor, sink = mixed[0:count // 2 * 2:2], mixed[1:count // 2 * 2:2]
    slack = jnp.minimum(lengths[donor] - 1, reach - lengths[sink]) // 2
    slack = jnp.where((donor == order[0]) | (sink == order[0]) | (lengths[sink] == 0), 0, jnp.maximum(slack, 0))
    passed = jax.random.randint(jax.random.fold_in(own, 4), (count // 2,), 0, 1 << 20) % (slack + 1)
    lengths = lengths.at[donor].add(-passed).at[sink].add(passed)
    members = jnp.searchsorted(jnp.cumsum(lengths), jnp.arange(rows * top), side="right").astype(jnp.int32)
    grid = members.reshape(top, rows).T
    grid = grid[jax.random.permutation(jax.random.fold_in(own, 1), rows)]
    rotation = jax.random.randint(jax.random.fold_in(own, 2), (rows, 1), 0, top)
    return jnp.take_along_axis(grid, (jnp.arange(top)[None, :] + rotation) % top, axis=1)


def portions_of(count, total, bound, lean, full):
    weights = [(1 << 20) // math.isqrt(grade ** lean) + 1 for grade in range(1, count + 1)]
    largest = bound if full else min(bound, max(-(-total // count), total * weights[0] // sum(weights)))
    least = 1 if total - largest >= count - 1 else 0
    counts, surplus = [largest] + [least] * (count - 1), total - largest - least * (count - 1)
    while surplus > 0:
        movable = [i for i in range(1, count) if counts[i] < largest] or [i for i in range(1, count) if counts[i] < bound]
        pool, budget = sum([weights[i] for i in movable]), surplus
        for i in movable:
            more = min(bound - counts[i], max(1, budget * weights[i] // pool), surplus)
            counts[i] = counts[i] + more
            surplus = surplus - more
    return np.array(counts)


def normal_values(rng, shape, spread, limit, split=(), kind=jnp.bfloat16):
    entries = spread * jax.random.normal(rng, shape, jnp.float32)
    if split:
        entries = entries * level_of(rng, shape, split, -0.22, 0.18)
    return jnp.clip(entries, -limit, limit).astype(kind)


def setup_inputs(seed: int = 0) -> dict:
    streams_of = jax.random.split(jax.random.key(seed), 11)
    replay = normal_values(streams_of[0], (EPISODES, EP_LEN, CELLS, CIN), 1.0, 6.0, ((0, 128),))
    instructions = normal_values(streams_of[1], (EPISODES, EMB), 1.0, 6.0, ((0, 128),))
    owners_keys = jax.random.split(jax.random.fold_in(streams_of[2], 1), FRAMES // FR_DEV)
    owners_turns = jax.random.permutation(jax.random.fold_in(streams_of[2], 3), FRAMES // FR_DEV)
    owners = jax.vmap(lambda own, number: routed_block(jax.random.fold_in(streams_of[2], 2), own, number, FR_DEV, N_DP, 1, CAPF, 2))(owners_keys, owners_turns).reshape((FRAMES, 1))
    episode_rows = set_ends(jax.random.randint(streams_of[3], (FRAMES,), 0, EP_DEV), jax.random.fold_in(streams_of[3], 1), 0, EP_DEV - 1).astype(jnp.int32)
    frame_steps = set_ends(jax.random.randint(streams_of[4], (FRAMES,), 0, EP_LEN), jax.random.fold_in(streams_of[4], 1), 0, EP_LEN - 1).astype(jnp.int32)
    w_expand = normal_values(streams_of[5], (CIN, HID), CIN ** -0.5, 0.375)
    dw_kernel = normal_values(streams_of[6], (9, HID), 9 ** -0.5, 2.0, (), jnp.float32)
    w_project = normal_values(streams_of[7], (HID, COUT), HID ** -0.5, 0.15625)
    film_weight = normal_values(streams_of[8], (EMB, 2 * COUT), EMB ** -0.5, 0.25)
    token_grad = normal_values(streams_of[9], (WINDOWS, STEPS, CELLS, COUT), (4.0 / (FR_DEV * CELLS * DEVICES) ** 0.5), 0.0390625, ((0, 128),))
    return {"replay": replay, "instructions": instructions, "owners": owners, "episode_rows": episode_rows, "frame_steps": frame_steps, "w_expand": w_expand, "dw_kernel": dw_kernel, "w_project": w_project, "film_weight": film_weight, "token_grad": token_grad}


def silu_parts(values):
    sigmoid_value = jax.nn.sigmoid(values)
    return values * sigmoid_value, sigmoid_value * (1.0 + values * (1.0 - sigmoid_value))


def depthwise(grid_values, dw_kernel):
    padded = jnp.pad(grid_values, ((0, 0), (1, 1), (1, 1), (0, 0)))
    result = jnp.zeros_like(grid_values)
    for kernel_tap in range(9):
        tap_row, tap_col = kernel_tap // 3, kernel_tap % 3
        result = result + dw_kernel[kernel_tap] * padded[:, tap_row:tap_row + SIDE, tap_col:tap_col + SIDE, :]
    return result


def depthwise_back(mixed_cot, source_grid, dw_kernel):
    padded_source = jnp.pad(source_grid, ((0, 0), (1, 1), (1, 1), (0, 0)))
    padded_cot = jnp.pad(mixed_cot, ((0, 0), (1, 1), (1, 1), (0, 0)))
    kernel_rows = []
    result = jnp.zeros_like(mixed_cot)
    for kernel_tap in range(9):
        tap_row, tap_col = kernel_tap // 3, kernel_tap % 3
        window = padded_source[:, tap_row:tap_row + SIDE, tap_col:tap_col + SIDE, :]
        kernel_rows.append(jnp.sum(mixed_cot * window, axis=(0, 1, 2)))
        result = result + dw_kernel[kernel_tap] * padded_cot[:, 2 - tap_row:2 - tap_row + SIDE, 2 - tap_col:2 - tap_col + SIDE, :]
    return jnp.stack(kernel_rows), result


def forward(frames, embedding, w_expand, dw_kernel, w_project, film_weight):
    amount, cell_count, in_width = frames.shape
    out_width = w_project.shape[1]
    before = jnp.dot(frames.reshape(amount * cell_count, in_width), w_expand, preferred_element_type=jnp.float32)
    first_hidden = lax.optimization_barrier(silu_parts(before)[0].astype(jnp.bfloat16))
    mixed = depthwise(first_hidden.astype(jnp.float32).reshape(amount, SIDE, SIDE, -1), dw_kernel)
    second_hidden = silu_parts(mixed)[0].astype(jnp.bfloat16).reshape(amount * cell_count, -1)
    projected = jnp.dot(second_hidden, w_project, preferred_element_type=jnp.float32).reshape(amount, cell_count, out_width)
    film_terms = jnp.dot(embedding, film_weight, preferred_element_type=jnp.float32)
    film_scale = 1.0 + film_terms[:, None, :out_width]
    film_shift = film_terms[:, None, out_width:]
    tokens = (film_scale * projected + film_shift).astype(jnp.bfloat16)
    return tokens, first_hidden.reshape(amount, cell_count, -1), projected


def backward(frames, embedding, first_hidden, projected, cotangent, w_expand, dw_kernel, w_project, film_weight):
    amount, cell_count, in_width = frames.shape
    out_width = w_project.shape[1]
    film_terms = jnp.dot(embedding, film_weight, preferred_element_type=jnp.float32)
    film_scale = 1.0 + film_terms[:, None, :out_width]
    upstream = cotangent.astype(jnp.float32)
    film_cot = jnp.concatenate([jnp.sum(upstream * projected, axis=1), jnp.sum(upstream, axis=1)], axis=1).astype(jnp.bfloat16)
    film_grad = jnp.dot(embedding.T, film_cot, preferred_element_type=jnp.float32)
    proj_cot = (upstream * film_scale).astype(jnp.bfloat16).reshape(amount * cell_count, out_width)
    first_grid = first_hidden.astype(jnp.float32).reshape(amount, SIDE, SIDE, -1)
    mixed = depthwise(first_grid, dw_kernel)
    second_act, second_slope = silu_parts(mixed)
    second_hidden = second_act.astype(jnp.bfloat16).reshape(amount * cell_count, -1)
    project_grad = jnp.dot(second_hidden.T, proj_cot, preferred_element_type=jnp.float32)
    second_cot = jnp.dot(proj_cot, w_project.T, preferred_element_type=jnp.float32)
    mixed_cot = second_cot.reshape(amount, SIDE, SIDE, -1) * second_slope
    kernel_grad, first_cot = depthwise_back(mixed_cot, first_grid, dw_kernel)
    flat_frames = frames.reshape(amount * cell_count, in_width)
    before = jnp.dot(flat_frames, w_expand, preferred_element_type=jnp.float32)
    first_slope = silu_parts(before)[1]
    pre_cot = (first_cot.reshape(amount * cell_count, -1) * first_slope).astype(jnp.bfloat16)
    expand_grad = jnp.dot(flat_frames.T, pre_cot, preferred_element_type=jnp.float32)
    return expand_grad, kernel_grad, project_grad, film_grad


def reference(replay, instructions, owners, episode_rows, frame_steps, w_expand, dw_kernel, w_project, film_weight, token_grad):
    frame_total = owners.shape[0]
    block_total = frame_total // FR_DEV
    requester = jnp.arange(frame_total, dtype=jnp.int32) // FR_DEV
    owner_block = owners[:, 0] * N_REPLICA + requester % N_REPLICA
    stored_rows = (owner_block * EP_DEV + episode_rows) * EP_LEN + frame_steps
    stored = replay.reshape(-1, CELLS, CIN)
    cotangents = token_grad.reshape(block_total, FR_DEV, CELLS, COUT)

    def one_block(totals, block_index):
        chosen = lax.dynamic_slice_in_dim(stored_rows, block_index * FR_DEV, FR_DEV)
        frames = jnp.take(stored, chosen, axis=0)
        embedding = jnp.take(instructions, chosen // EP_LEN, axis=0)
        tokens, first_hidden, projected = forward(frames, embedding, w_expand, dw_kernel, w_project, film_weight)
        fresh = backward(frames, embedding, first_hidden, projected, cotangents[block_index], w_expand, dw_kernel, w_project, film_weight)
        return tuple(left + right for left, right in zip(totals, fresh)), tokens

    start_totals = (jnp.zeros(w_expand.shape, jnp.float32), jnp.zeros(dw_kernel.shape, jnp.float32), jnp.zeros(w_project.shape, jnp.float32), jnp.zeros(film_weight.shape, jnp.float32))
    gradients, tokens = lax.scan(one_block, start_totals, jnp.arange(block_total, dtype=jnp.int32))
    return (tokens.reshape(token_grad.shape), gradients[0], gradients[1], gradients[2], gradients[3])
```

```python
import jax, jax.numpy as jnp
from jax import lax
from jax.experimental import pallas as pl
from jax.experimental.pallas import tpu as pltpu
from jax.sharding import PartitionSpec as P

SIDE, CELLS, TILE = 9, 81, 8
CIN, HID, COUT, EMB, FR = 232, 1392, 384, 512, 36
HP = 1408
NT = 5
ROWS = CELLS * TILE
f32, bf16 = jnp.float32, jnp.bfloat16


def vpu_block(lane, tile_pre, tile_sc, dw_ref, F, S1, M, sec, prec, gk_ref):
    ln = pl.ds(lane, 128)
    row = lambda c: slice(c * 8, c * 8 + 8)
    for c in range(CELLS):
        h = tile_pre[row(c), ln]
        t = jnp.tanh(h)
        u = 1.0 + t
        F[row(c), :] = h * u
        S1[row(c), :] = u * (1.0 + h * (1.0 - t))
    taps = [dw_ref[t * 8:t * 8 + 8, ln] for t in range(9)]
    acc = [gk_ref[t * 8:t * 8 + 8, ln] for t in range(9)]
    get = lambda ref, i: [ref[row(i * 9 + k), :] for k in range(9)]
    prev, cur, nxt = None, None, get(F, 0)
    for i in range(9):
        prev, cur = cur, nxt
        nxt = get(F, i + 1) if i < 8 else None
        rows3 = (prev, cur, nxt)
        for k in range(9):
            total = None
            for r in range(3):
                if rows3[r] is None:
                    continue
                for c in range(3):
                    kk = k + c - 1
                    if 0 <= kk < 9:
                        term = taps[3 * r + c] * rows3[r][kk]
                        total = term if total is None else total + term
            h = total
            t = jnp.tanh(h)
            u = 1.0 + t
            sec[row(i * 9 + k), ln] = h * u
            mc = tile_sc[row(i * 9 + k), ln] * (u * (1.0 + h * (1.0 - t)))
            M[row(i * 9 + k), :] = mc
            for r in range(3):
                if rows3[r] is None:
                    continue
                for c in range(3):
                    kk = k + c - 1
                    if 0 <= kk < 9:
                        acc[3 * r + c] = acc[3 * r + c] + mc * rows3[r][kk]
    for t in range(9):
        gk_ref[t * 8:t * 8 + 8, ln] = acc[t]
    prev, cur, nxt = None, None, get(M, 0)
    for i in range(9):
        prev, cur = cur, nxt
        nxt = get(M, i + 1) if i < 8 else None
        rows3 = (nxt, cur, prev)
        for k in range(9):
            total = None
            for r in range(3):
                if rows3[r] is None:
                    continue
                for c in range(3):
                    kk = k - c + 1
                    if 0 <= kk < 9:
                        term = taps[3 * r + c] * rows3[r][kk]
                        total = term if total is None else total + term
            prec[row(i * 9 + k), ln] = total * S1[row(i * 9 + k), :]


def kernel(x_ref, e_ref, g_ref, we_ref, dw_ref, wp_ref, wpt_ref, fw_ref,
           tok_ref, ge_ref, gk_ref, gp_ref, gf_ref,
           x32, xb, g32, pc, film, pre, sc, sec, prec, secb, precb, proj, F, S1, M, fc, gpt):
    film[...] = jnp.dot(e_ref[...], fw_ref[...], preferred_element_type=f32)
    gk_ref[...] = jnp.zeros_like(gk_ref)
    ge_ref[...] = jnp.zeros_like(ge_ref)
    gpt[...] = jnp.zeros_like(gpt)

    def tile(ft, carry):
        for f in range(TILE):
            for l in range(2):
                x32[l, pl.ds(f, CELLS, stride=TILE), :] = x_ref[ft * TILE + f, :, l * 128:l * 128 + 128].astype(f32)
            for l in range(3):
                g32[l, pl.ds(f, CELLS, stride=TILE), :] = g_ref[ft * TILE + f, :, l * 128:l * 128 + 128].astype(f32)
        for l in range(2):
            xb[:, l * 128:l * 128 + 128] = x32[l].astype(bf16)
        fm = film[pl.ds(pl.multiple_of(ft * TILE, TILE), TILE), :]
        scale, shift = 1.0 + fm[:, :COUT], fm[:, COUT:]
        for l in range(3):
            sl = slice(l * 128, l * 128 + 128)
            pc[:, sl] = (g32[l].reshape(CELLS, TILE, 128) * scale[None, :, sl]).reshape(ROWS, 128).astype(bf16)
        pre[...] = jnp.dot(xb[...], we_ref[...], preferred_element_type=f32)
        sc[...] = jnp.dot(pc[...], wpt_ref[...], preferred_element_type=f32)

        def lanes(lt, carry):
            vpu_block(pl.multiple_of(lt * 128, 128), pre, sc, dw_ref, F, S1, M, sec, prec, gk_ref)
            return carry
        lax.fori_loop(0, HP // 128, lanes, 0)
        secb[...] = sec[...].astype(bf16)
        precb[...] = prec[...].astype(bf16)
        pj = jnp.dot(secb[...], wp_ref[...], preferred_element_type=f32)
        fr = pl.ds(pl.multiple_of(ft * TILE, TILE), TILE)
        for l in range(3):
            sl = slice(l * 128, l * 128 + 128)
            g3, pj3 = g32[l].reshape(CELLS, TILE, 128), pj[:, sl].reshape(CELLS, TILE, 128)
            fc[fr, sl] = jnp.sum(g3 * pj3, axis=0)
            fc[fr, COUT + l * 128:COUT + l * 128 + 128] = jnp.sum(g3, axis=0)
            proj[l] = (pj3 * scale[None, :, sl] + shift[None, :, sl]).reshape(ROWS, 128)
        for f in range(TILE):
            for l in range(3):
                tok_ref[ft * TILE + f, :, l * 128:l * 128 + 128] = proj[l, pl.ds(f, CELLS, stride=TILE), :].astype(bf16)
        tn = (((0,), (0,)), ((), ()))
        ge_ref[...] += lax.dot_general(xb[...], precb[...], tn, preferred_element_type=f32)
        gpt[...] += lax.dot_general(pc[...], secb[...], tn, preferred_element_type=f32)
        return carry
    lax.fori_loop(0, NT, tile, 0)
    gp_ref[...] = gpt[...].T
    gf_ref[...] = lax.dot_general(e_ref[...], fc[...].astype(bf16), (((0,), (0,)), ((), ())), preferred_element_type=f32)


def compute(frames, emb, g, w_expand, dw_kernel, w_project, film_weight):
    x = jnp.pad(frames, ((0, 4), (0, 0), (0, 24)))
    e = jnp.pad(emb, ((0, 4), (0, 0)))
    gg = jnp.pad(g, ((0, 4), (0, 0), (0, 0)))
    we = jnp.pad(w_expand * jnp.asarray(0.5, bf16), ((0, 24), (0, 16)))
    wp = jnp.pad(w_project, ((0, 16), (0, 0)))
    wpt = jnp.pad((w_project * jnp.asarray(0.5, bf16)).T, ((0, 0), (0, 16)))
    dw = jnp.repeat(jnp.pad(dw_kernel * 0.5, ((0, 0), (0, 16))), 8, axis=0)
    V = pl.BlockSpec(memory_space=pltpu.VMEM)
    S = lambda r, c, t=f32: pltpu.VMEM((r, c), t)
    tok, ge, gk, gp, gf = pl.pallas_call(
        kernel,
        out_shape=(jax.ShapeDtypeStruct((40, CELLS, COUT), bf16), jax.ShapeDtypeStruct((256, HP), f32),
                   jax.ShapeDtypeStruct((72, HP), f32), jax.ShapeDtypeStruct((HP, COUT), f32),
                   jax.ShapeDtypeStruct((EMB, 2 * COUT), f32)),
        in_specs=[V] * 8, out_specs=(V,) * 5,
        scratch_shapes=[pltpu.VMEM((2, ROWS, 128), f32), S(ROWS, 256, bf16), pltpu.VMEM((3, ROWS, 128), f32), S(ROWS, COUT, bf16), S(40, 2 * COUT),
                        S(ROWS, HP), S(ROWS, HP), S(ROWS, HP), S(ROWS, HP), S(ROWS, HP, bf16), S(ROWS, HP, bf16), pltpu.VMEM((3, ROWS, 128), f32),
                        S(ROWS, 128), S(ROWS, 128), S(ROWS, 128), S(40, 2 * COUT), S(COUT, HP)],
        compiler_params=pltpu.CompilerParams(vmem_limit_bytes=60 * 2**20),
    )(x, e, gg, we, dw, wp, wpt, film_weight)
    gk = gk.reshape(9, 8, HP).sum(axis=1)[:, :HID]
    return tok[:FR], ge[:CIN, :HID], gk, gp[:HID], gf


def per_device(
    replay,
    instructions,
    owners,
    episode_rows,
    frame_steps,
    w_expand,
    dw_kernel,
    w_project,
    film_weight,
    token_grad,
):
    peer_count = lax.axis_size("dp")
    frame_count = owners.shape[0]
    capacity = max(2, (2 * frame_count + peer_count - 1) // peer_count)
    slot_count = peer_count * capacity
    episode_length = replay.shape[1]
    cell_count = replay.shape[2]
    out_width = w_project.shape[1]
    owner_ids = owners[:, 0]
    positions = jnp.arange(frame_count, dtype=jnp.int32)
    earlier = (owner_ids[:, None] == owner_ids[None, :]) & (positions[:, None] < positions[None, :])
    rank_within = jnp.sum(earlier.astype(jnp.int32), axis=0)
    target = owner_ids * capacity + rank_within
    onehot = target[:, None] == jnp.arange(slot_count, dtype=jnp.int32)[None, :]
    wanted = episode_rows * episode_length + frame_steps
    request = jnp.sum(jnp.where(onehot, wanted[:, None], 0), axis=0).reshape(peer_count, capacity)
    asked_rows = lax.all_to_all(request, "dp", split_axis=0, concat_axis=0, tiled=True).reshape(
        slot_count
    )
    stored = replay.reshape(-1, cell_count, replay.shape[3])
    picked = jnp.take(stored, asked_rows, axis=0)
    picked_embedding = jnp.take(instructions, asked_rows // episode_length, axis=0)
    arrived, arrived_embedding = (
        lax.all_to_all(
            picked.reshape(peer_count, capacity, cell_count, -1),
            "dp",
            split_axis=0,
            concat_axis=0,
            tiled=True,
        ),
        lax.all_to_all(
            picked_embedding.reshape(peer_count, capacity, -1),
            "dp",
            split_axis=0,
            concat_axis=0,
            tiled=True,
        ),
    )
    frames = jnp.take(arrived.reshape(slot_count, cell_count, -1), target, axis=0)
    embedding = jnp.take(arrived_embedding.reshape(slot_count, -1), target, axis=0)
    cotangent = token_grad.reshape(frame_count, cell_count, out_width)
    tokens, *gradients = compute(
        frames, embedding, cotangent, w_expand, dw_kernel, w_project, film_weight
    )
    tokens_out = tokens.reshape(token_grad.shape)
    summed = lax.psum(tuple(gradients), ("dp", "replica"))
    return (tokens_out, summed[0], summed[1], summed[2], summed[3])


def solution(mesh):
    in_specs = (
        P(("dp", "replica"), None, None, None),
        P(("dp", "replica"), None),
        P(("dp", "replica"), None),
        P(("dp", "replica")),
        P(("dp", "replica")),
        P(),
        P(),
        P(),
        P(),
        P(("dp", "replica"), None, None, None),
    )
    out_specs = (P(("dp", "replica"), None, None, None), P(), P(), P(), P())
    return jax.shard_map(
        per_device, mesh=mesh, in_specs=in_specs, out_specs=out_specs, check_vma=False
    )
```

```python
import jax, jax.numpy as jnp
from jax import lax
from jax.experimental import pallas as pl
from jax.experimental.pallas import tpu as pltpu
from jax.sharding import PartitionSpec as P

SIDE, CELLS, TILE = 9, 81, 8
CIN, HID, COUT, EMB, FR = 232, 1392, 384, 512, 36
HP = 1408
NT = 5
GR = 10240
GE, GK, GP, GF = 0, 2640, 2816, 6992
ROWS = CELLS * TILE
f32, bf16 = jnp.float32, jnp.bfloat16


def vpu_block(lane, tile_pre, tile_sc, dw_ref, F, S1, M, sec, prec, gk_ref):
    ln = pl.ds(lane, 128)
    row = lambda c: slice(c * 8, c * 8 + 8)
    for c in range(CELLS):
        h = tile_pre[row(c), ln]
        t = jnp.tanh(h)
        u = 1.0 + t
        F[row(c), :] = h * u
        S1[row(c), :] = u * (1.0 + h * (1.0 - t))
    taps = [dw_ref[t * 8:t * 8 + 8, ln] for t in range(9)]
    acc = [gk_ref[t * 8:t * 8 + 8, ln] for t in range(9)]
    get = lambda ref, i: [ref[row(i * 9 + k), :] for k in range(9)]
    prev, cur, nxt = None, None, get(F, 0)
    for i in range(9):
        prev, cur = cur, nxt
        nxt = get(F, i + 1) if i < 8 else None
        rows3 = (prev, cur, nxt)
        for k in range(9):
            total = None
            for r in range(3):
                if rows3[r] is None:
                    continue
                for c in range(3):
                    kk = k + c - 1
                    if 0 <= kk < 9:
                        term = taps[3 * r + c] * rows3[r][kk]
                        total = term if total is None else total + term
            h = total
            t = jnp.tanh(h)
            u = 1.0 + t
            sec[row(i * 9 + k), ln] = h * u
            mc = tile_sc[row(i * 9 + k), ln] * (u * (1.0 + h * (1.0 - t)))
            M[row(i * 9 + k), :] = mc
            for r in range(3):
                if rows3[r] is None:
                    continue
                for c in range(3):
                    kk = k + c - 1
                    if 0 <= kk < 9:
                        acc[3 * r + c] = acc[3 * r + c] + mc * rows3[r][kk]
    for t in range(9):
        gk_ref[t * 8:t * 8 + 8, ln] = acc[t]
    prev, cur, nxt = None, None, get(M, 0)
    for i in range(9):
        prev, cur = cur, nxt
        nxt = get(M, i + 1) if i < 8 else None
        rows3 = (nxt, cur, prev)
        for k in range(9):
            total = None
            for r in range(3):
                if rows3[r] is None:
                    continue
                for c in range(3):
                    kk = k - c + 1
                    if 0 <= kk < 9:
                        term = taps[3 * r + c] * rows3[r][kk]
                        total = term if total is None else total + term
            prec[row(i * 9 + k), ln] = total * S1[row(i * 9 + k), :]


def kernel(x_ref, e_ref, g_ref, we_ref, dw_ref, wp_ref, wpt_ref, fw_ref,
           tok_ref, sum_ref,
           x32, xb, g32, pc, film, pre, sc, sec, prec, secb, precb, proj, F, S1, M, fc, gpt, ge_ref, gk_ref):
    film[FR:, :] = jnp.zeros((NT * TILE - FR, 2 * COUT), f32)
    film[:FR, :] = jnp.dot(e_ref[...], fw_ref[...], preferred_element_type=f32)
    gk_ref[...] = jnp.zeros_like(gk_ref)
    ge_ref[...] = jnp.zeros_like(ge_ref)
    gpt[...] = jnp.zeros_like(gpt)

    def tile(ft, carry):
        for f in range(TILE):
            j = ft * TILE + f
            held, keep = jnp.minimum(j, FR - 1), jnp.where(j < FR, 1.0, 0.0)
            for l in range(2):
                x32[l, pl.ds(f, CELLS, stride=TILE), :] = x_ref[held, :, l * 128:l * 128 + 128].astype(f32) * keep
            for l in range(3):
                g32[l, pl.ds(f, CELLS, stride=TILE), :] = g_ref[held, :, l * 128:l * 128 + 128].astype(f32) * keep
        for l in range(2):
            xb[:, l * 128:l * 128 + 128] = x32[l].astype(bf16)
        fm = film[pl.ds(pl.multiple_of(ft * TILE, TILE), TILE), :]
        scale, shift = 1.0 + fm[:, :COUT], fm[:, COUT:]
        for l in range(3):
            sl = slice(l * 128, l * 128 + 128)
            pc[:, sl] = (g32[l].reshape(CELLS, TILE, 128) * scale[None, :, sl]).reshape(ROWS, 128).astype(bf16)
        pre[...] = jnp.dot(xb[...], we_ref[...], preferred_element_type=f32)
        sc[...] = jnp.dot(pc[...], wpt_ref[...], preferred_element_type=f32)

        def lanes(lt, carry):
            vpu_block(pl.multiple_of(lt * 128, 128), pre, sc, dw_ref, F, S1, M, sec, prec, gk_ref)
            return carry
        lax.fori_loop(0, HP // 128, lanes, 0)
        secb[...] = sec[...].astype(bf16)
        precb[...] = prec[...].astype(bf16)
        pj = jnp.dot(secb[...], wp_ref[...], preferred_element_type=f32)
        fr = pl.ds(pl.multiple_of(ft * TILE, TILE), TILE)
        for l in range(3):
            sl = slice(l * 128, l * 128 + 128)
            g3, pj3 = g32[l].reshape(CELLS, TILE, 128), pj[:, sl].reshape(CELLS, TILE, 128)
            fc[fr, sl] = jnp.sum(g3 * pj3, axis=0)
            fc[fr, COUT + l * 128:COUT + l * 128 + 128] = jnp.sum(g3, axis=0)
            proj[l] = (pj3 * scale[None, :, sl] + shift[None, :, sl]).reshape(ROWS, 128)
        for f in range(TILE):
            @pl.when(ft * TILE + f < FR)
            def _(f=f):
                for l in range(3):
                    tok_ref[ft * TILE + f, :, l * 128:l * 128 + 128] = proj[l, pl.ds(f, CELLS, stride=TILE), :].astype(bf16)
        tn = (((0,), (0,)), ((), ()))
        ge_ref[...] += lax.dot_general(xb[...], precb[...], tn, preferred_element_type=f32)
        gpt[...] += lax.dot_general(pc[...], secb[...], tn, preferred_element_type=f32)
        return carry
    lax.fori_loop(0, NT, tile, 0)
    gk = jnp.concatenate([jnp.sum(gk_ref[...].reshape(9, 8, HP), axis=1), jnp.zeros((7, HP), f32)], axis=0).astype(bf16)
    for lt in range(HP // 128):
        ln = slice(lt * 128, lt * 128 + 128)
        sum_ref[GE + lt * 240:GE + lt * 240 + 240, :] = ge_ref[:240, ln].astype(bf16)
        sum_ref[GK + lt * 16:GK + lt * 16 + 16, :] = gk[:, ln]
    for l in range(3):
        sum_ref[GP + l * HID:GP + l * HID + HID, :] = gpt[l * 128:l * 128 + 128, :].T[:HID].astype(bf16)
    gf = lax.dot_general(e_ref[...], fc[:FR, :].astype(bf16), (((0,), (0,)), ((), ())), preferred_element_type=f32).astype(bf16)
    for l in range(6):
        sum_ref[GF + l * EMB:GF + l * EMB + EMB, :] = gf[:, l * 128:l * 128 + 128]
    sum_ref[GF + 6 * EMB:, :] = jnp.zeros((GR - GF - 6 * EMB, 128), bf16)


def compute(frames, emb, g, w_expand, dw_kernel, w_project, film_weight):
    x = jnp.pad(frames, ((0, 0), (0, 0), (0, 24)))
    we = jnp.pad(w_expand * jnp.asarray(0.5, bf16), ((0, 24), (0, 16)))
    wp = jnp.pad(w_project, ((0, 16), (0, 0)))
    wpt = jnp.pad((w_project * jnp.asarray(0.5, bf16)).T, ((0, 0), (0, 16)))
    dw = jnp.repeat(jnp.pad(dw_kernel * 0.5, ((0, 0), (0, 16))), 8, axis=0)
    V = pl.BlockSpec(memory_space=pltpu.VMEM)
    S = lambda r, c, t=f32: pltpu.VMEM((r, c), t)
    return pl.pallas_call(
        kernel,
        out_shape=(jax.ShapeDtypeStruct((FR, CELLS, COUT), bf16), jax.ShapeDtypeStruct((GR, 128), bf16)),
        in_specs=[V] * 8, out_specs=(V,) * 2,
        scratch_shapes=[pltpu.VMEM((2, ROWS, 128), f32), S(ROWS, 256, bf16), pltpu.VMEM((3, ROWS, 128), f32), S(ROWS, COUT, bf16), S(NT * TILE, 2 * COUT),
                        S(ROWS, HP), S(ROWS, HP), S(ROWS, HP), S(ROWS, HP), S(ROWS, HP, bf16), S(ROWS, HP, bf16), pltpu.VMEM((3, ROWS, 128), f32),
                        S(ROWS, 128), S(ROWS, 128), S(ROWS, 128), S(NT * TILE, 2 * COUT), S(COUT, HP), S(256, HP), S(72, HP)],
        compiler_params=pltpu.CompilerParams(vmem_limit_bytes=60 * 2**20),
        name="film_block",
    )(x, emb, g, we, dw, wp, wpt, film_weight)


PIECES = (32, 32, 16)
STARTS = (0, 4096, 8192)
ORDERS = (("x", "y", "z"), ("y", "z", "x"), ("z", "x", "y"))


def place():
    dp, rep = lax.axis_index("dp"), lax.axis_index("replica")
    return {"x": rep, "y": dp // 8, "z": (dp // 2) % 4, "core": dp % 2}


def device_of(at):
    return ((at["y"] * 4 + at["z"]) * 2 + at["core"], at["x"])


def shifted(at, axis, d):
    size = 2 if axis == "core" else 4
    other = dict(at)
    other[axis] = (at[axis] + d) % size
    return other


def reduce_kernel(g_ref, ge_ref, gk_ref, gp_ref, gf_ref, total, part, r0, r1, r2, r3, send, recv):
    at = place()
    barrier = pltpu.get_barrier_semaphore()
    peers = [shifted(at, "core", 1)] + [shifted(at, a, d) for a in "xyz" for d in (1, 2, 3)]
    for p in peers:
        pl.semaphore_signal(barrier, inc=1, device_id=device_of(p), device_id_type=pl.DeviceIdType.MESH)
    pl.semaphore_wait(barrier, len(peers))
    land = (r0, r1, r2, r3)
    waits = []

    def push(src, dst, stage, s, d, peer):
        copy = pltpu.make_async_remote_copy(src_ref=src, dst_ref=dst, send_sem=send.at[stage, s, d], recv_sem=recv.at[stage, s, d],
                                            device_id=device_of(peer), device_id_type=pl.DeviceIdType.MESH)
        copy.start()
        waits.append(copy)
        return copy

    def span(base, index, rows):
        return pl.ds(pl.multiple_of(base + index * rows, 16), rows)

    state = []
    for s, r in enumerate(PIECES):
        base, half = STARTS[s], 64 * r
        peer = shifted(at, "core", 1)
        c = push(g_ref.at[span(base, peer["core"], half)], r0.at[pl.ds(base // 2, half)], 0, s, 0, peer)
        state.append([c])
    for stage in (1, 2, 3):
        for s, r in enumerate(PIECES):
            axis = ORDERS[s][stage - 1]
            have = r * 4 ** (4 - stage)
            base = STARTS[s] // 2
            for c in state[s]:
                c.wait_recv()
            if stage == 1:
                mine = g_ref[span(STARTS[s], at["core"], have)].astype(f32) + r0[pl.ds(base, have)].astype(f32)
            else:
                prev = land[stage - 1]
                pb = base // 4 ** (stage - 1)
                old = part[stage - 2, span(base, at[ORDERS[s][stage - 2]], have)].astype(f32)
                mine = old
                for d in (1, 2, 3):
                    mine = mine + prev[d - 1, pl.ds(pb, have)].astype(f32)
            part[stage - 1, pl.ds(base, have)] = mine.astype(bf16)
            block = have // 4
            state[s] = []
            for d in (1, 2, 3):
                peer = shifted(at, axis, d)
                state[s].append(push(part.at[stage - 1, span(base, peer[axis], block)],
                                     land[stage].at[d - 1, pl.ds(base // 4 ** stage, block)], stage, s, d - 1, peer))
    where = []
    for s, r in enumerate(PIECES):
        for c in state[s]:
            c.wait_recv()
        base = STARTS[s] // 2
        mine = part[2, span(base, at[ORDERS[s][2]], r)].astype(f32)
        for d in (1, 2, 3):
            mine = mine + r3[d - 1, pl.ds(base // 64, r)].astype(f32)
        a1, a2, a3 = ORDERS[s]
        index = ((at["core"] * 4 + at[a1]) * 4 + at[a2]) * 4 + at[a3]
        where.append(index)
        total[span(STARTS[s], index, r)] = mine.astype(bf16)
        state[s] = []
        for d in (1, 2, 3):
            sl = span(STARTS[s], index, r)
            state[s].append(push(total.at[sl], total.at[sl], 4, s, d - 1, shifted(at, a3, d)))
    for stage in (5, 6, 7):
        for s, r in enumerate(PIECES):
            for c in state[s]:
                c.wait_recv()
            rows = r * 4 ** (stage - 4)
            index = where[s] // 4 ** (stage - 4)
            sl = span(STARTS[s], index, rows)
            state[s] = []
            if stage == 7:
                state[s].append(push(total.at[sl], total.at[sl], stage, s, 0, shifted(at, "core", 1)))
            else:
                axis = ORDERS[s][6 - stage]
                for d in (1, 2, 3):
                    state[s].append(push(total.at[sl], total.at[sl], stage, s, d - 1, shifted(at, axis, d)))
    for s in range(3):
        for c in state[s]:
            c.wait_recv()
    for c in waits:
        c.wait_send()
    for lt in range(11):
        w = min(128, HID - lt * 128)
        ge_ref[:, lt * 128:lt * 128 + w] = total[GE + lt * 240:GE + lt * 240 + 240].astype(f32)[:CIN, :w]
        gk_ref[:, lt * 128:lt * 128 + w] = total[GK + lt * 16:GK + lt * 16 + 16].astype(f32)[:9, :w]
    for l in range(3):
        gp_ref[:, l * 128:l * 128 + 128] = total[GP + l * HID:GP + l * HID + HID].astype(f32)
    for l in range(6):
        gf_ref[:, l * 128:l * 128 + 128] = total[GF + l * EMB:GF + l * EMB + EMB].astype(f32)


def all_reduce(g):
    V = pl.BlockSpec(memory_space=pltpu.VMEM)
    return pl.pallas_call(
        reduce_kernel,
        out_shape=(jax.ShapeDtypeStruct((CIN, HID), f32), jax.ShapeDtypeStruct((9, HID), f32),
                   jax.ShapeDtypeStruct((HID, COUT), f32), jax.ShapeDtypeStruct((EMB, 2 * COUT), f32)),
        in_specs=[V], out_specs=(V,) * 4,
        scratch_shapes=[pltpu.VMEM((GR, 128), bf16), pltpu.VMEM((3, GR // 2, 128), bf16), pltpu.VMEM((GR // 2, 128), bf16),
                        pltpu.VMEM((3, GR // 8, 128), bf16), pltpu.VMEM((3, GR // 32, 128), bf16), pltpu.VMEM((3, GR // 128, 128), bf16),
                        pltpu.SemaphoreType.DMA((8, 3, 3)), pltpu.SemaphoreType.DMA((8, 3, 3))],
        compiler_params=pltpu.CompilerParams(vmem_limit_bytes=48 * 2**20, collective_id=1, has_side_effects=True),
        name="grad_sum",
    )(g)


def per_device(
    replay,
    instructions,
    owners,
    episode_rows,
    frame_steps,
    w_expand,
    dw_kernel,
    w_project,
    film_weight,
    token_grad,
):
    peer_count = lax.axis_size("dp")
    frame_count = owners.shape[0]
    capacity = max(2, (2 * frame_count + peer_count - 1) // peer_count)
    slot_count = peer_count * capacity
    episode_length = replay.shape[1]
    cell_count = replay.shape[2]
    out_width = w_project.shape[1]
    owner_ids = owners[:, 0]
    positions = jnp.arange(frame_count, dtype=jnp.int32)
    earlier = (owner_ids[:, None] == owner_ids[None, :]) & (positions[:, None] < positions[None, :])
    rank_within = jnp.sum(earlier.astype(jnp.int32), axis=0)
    target = owner_ids * capacity + rank_within
    onehot = target[:, None] == jnp.arange(slot_count, dtype=jnp.int32)[None, :]
    wanted = episode_rows * episode_length + frame_steps
    request = jnp.sum(jnp.where(onehot, wanted[:, None], 0), axis=0).reshape(peer_count, capacity)
    asked_rows = lax.all_to_all(request, "dp", split_axis=0, concat_axis=0, tiled=True).reshape(
        slot_count
    )
    stored = replay.reshape(-1, cell_count, replay.shape[3])
    picked = jnp.take(stored, asked_rows, axis=0)
    picked_embedding = jnp.take(instructions, asked_rows // episode_length, axis=0)
    arrived, arrived_embedding = (
        lax.all_to_all(
            picked.reshape(peer_count, capacity, cell_count, -1),
            "dp",
            split_axis=0,
            concat_axis=0,
            tiled=True,
        ),
        lax.all_to_all(
            picked_embedding.reshape(peer_count, capacity, -1),
            "dp",
            split_axis=0,
            concat_axis=0,
            tiled=True,
        ),
    )
    frames = jnp.take(arrived.reshape(slot_count, cell_count, -1), target, axis=0)
    embedding = jnp.take(arrived_embedding.reshape(slot_count, -1), target, axis=0)
    cotangent = token_grad.reshape(frame_count, cell_count, out_width)
    tokens, partial_sums = compute(
        frames, embedding, cotangent, w_expand, dw_kernel, w_project, film_weight
    )
    tokens_out = tokens.reshape(token_grad.shape)
    summed = all_reduce(partial_sums)
    return (tokens_out, summed[0], summed[1], summed[2], summed[3])


def solution(mesh):
    in_specs = (
        P(("dp", "replica"), None, None, None),
        P(("dp", "replica"), None),
        P(("dp", "replica"), None),
        P(("dp", "replica")),
        P(("dp", "replica")),
        P(),
        P(),
        P(),
        P(),
        P(("dp", "replica"), None, None, None),
    )
    out_specs = (P(("dp", "replica"), None, None, None), P(), P(), P(), P())
    return jax.shard_map(
        per_device, mesh=mesh, in_specs=in_specs, out_specs=out_specs, check_vma=False
    )
```

```python
import functools
import jax, jax.numpy as jnp
from jax import lax
from jax.experimental import pallas as pl
from jax.experimental.pallas import tpu as pltpu
from jax.sharding import PartitionSpec as P

SIDE, CELLS, TILE = 9, 81, 8
CIN, HID, COUT, EMB, FR = 232, 1392, 384, 512, 36
HP = 1408
NT = 5
ROWS = CELLS * TILE
PEERS, RANKS, SLOT = 32, 3, 176
EP_DEV, EP_LEN = 8, 24
GR = 10240
GE, GK, GP, GF = 0, 2640, 2816, 6992
f32, bf16 = jnp.float32, jnp.bfloat16


def fetch_kernel(ask_ref, rep_ref, ins_ref, got_ref, later_ref,
                 rep, asks, stage, out, got, rep_sem, ask_send, ask_recv, send, recv):
    me, rail = lax.axis_index("dp"), lax.axis_index("replica")
    load = pltpu.make_async_copy(rep_ref, rep, rep_sem)
    load.start()
    barrier = pltpu.get_barrier_semaphore()

    def peer(d):
        return lax.rem(me + d, PEERS)

    def greet(d, c):
        pl.semaphore_signal(barrier, inc=1, device_id=(peer(d), rail), device_id_type=pl.DeviceIdType.MESH)
        return c
    lax.fori_loop(1, PEERS, greet, 0)
    pl.semaphore_wait(barrier, PEERS - 1)

    def ask(d):
        return pltpu.make_async_remote_copy(src_ref=ask_ref, dst_ref=asks.at[me], send_sem=ask_send.at[d], recv_sem=ask_recv.at[d],
                                            device_id=(peer(d), rail), device_id_type=pl.DeviceIdType.MESH)

    def frame(d):
        return pltpu.make_async_remote_copy(src_ref=out.at[peer(d)], dst_ref=got.at[me], send_sem=send.at[d], recv_sem=recv.at[d],
                                            device_id=(peer(d), rail), device_id_type=pl.DeviceIdType.MESH)

    def each(f):
        def body(d, c):
            f(d)
            return c
        lax.fori_loop(1, PEERS, body, 0)
    each(lambda d: ask(d).start())
    asks[me] = ask_ref[...]
    zero = jnp.zeros((PEERS * RANKS, 128), f32)
    for r in range(2 * CELLS + 4, SLOT):
        stage[pl.ds(r, PEERS * RANKS, stride=SLOT), :] = zero
    each(lambda d: ask(d).wait_recv())
    owner, wanted = asks[:, 0, :], asks[:, 1, :]
    mine = owner == me
    before = lax.broadcasted_iota(jnp.int32, (128, 128), 0) < lax.broadcasted_iota(jnp.int32, (128, 128), 1)
    rank = jnp.dot(jnp.where(mine, 1.0, 0.0).astype(bf16), jnp.where(before, 1.0, 0.0).astype(bf16), preferred_element_type=f32)
    wide = wanted.astype(f32)
    picks = []
    for k in range(RANKS):
        hit = mine & (rank > k - 0.5) & (rank < k + 0.5)
        picks.append(jnp.sum(jnp.where(hit, wide + 1.0, 0.0), axis=1, keepdims=True) - 1.0)
    pick = jnp.concatenate(picks, axis=0)
    at = lax.broadcasted_iota(jnp.int32, (PEERS * RANKS, EP_DEV * EP_LEN), 1).astype(f32)
    choose = jnp.where(pick == at, 1.0, 0.0).astype(bf16)
    low = lax.broadcasted_iota(jnp.int32, (PEERS * RANKS, EP_DEV), 1).astype(f32) * EP_LEN
    which = jnp.where((pick >= low) & (pick < low + EP_LEN), 1.0, 0.0).astype(bf16)
    words = jnp.dot(which, ins_ref[...], preferred_element_type=f32)

    def put(row, values):
        stage[pl.ds(row, PEERS, stride=SLOT), :] = values[:PEERS]

    def put_later(row, values):
        for k in range(2):
            stage[pl.ds((PEERS + k) * SLOT + row, PEERS, stride=2 * SLOT), :] = values[k * PEERS:k * PEERS + PEERS]
    for q in range(4):
        put(2 * CELLS + q, words[:PEERS, q * 128:q * 128 + 128])
        put_later(2 * CELLS + q, words[PEERS:, q * 128:q * 128 + 128])
    load.wait()

    def cells(chosen, store):
        blank = jnp.zeros((chosen.shape[0], 256 - CIN), f32)

        def some(i, carry):
            for u in range(3):
                c = i * 3 + u
                found = jnp.dot(chosen, rep[:, c].reshape(EP_DEV * EP_LEN, CIN), preferred_element_type=f32)
                store(c, found[:, :128])
                store(CELLS + c, jnp.concatenate([found[:, 128:], blank], axis=1))
            return carry
        lax.fori_loop(0, CELLS // 3, some, 0)
    cells(choose[:PEERS], put)

    def pack(p, carry):
        out[p] = stage[pl.ds(pl.multiple_of(p * SLOT, 8), SLOT), :].astype(bf16)
        return carry
    lax.fori_loop(0, PEERS, pack, 0)
    each(lambda d: frame(d).start())
    got[me] = out[me]
    cells(choose[PEERS:], put_later)

    def pack_later(p, carry):
        later_ref[p] = stage[pl.ds(pl.multiple_of((PEERS + p) * SLOT, 8), SLOT), :].astype(bf16)
        return carry
    lax.fori_loop(0, 2 * PEERS, pack_later, 0)
    each(lambda d: ask(d).wait_send())
    each(lambda d: frame(d).wait_recv())
    got_ref[...] = got[...]
    each(lambda d: frame(d).wait_send())


def fetch(asks, replay, instructions):
    V = pl.BlockSpec(memory_space=pltpu.VMEM)
    return pl.pallas_call(
        fetch_kernel,
        out_shape=(jax.ShapeDtypeStruct((PEERS, SLOT, 128), bf16), jax.ShapeDtypeStruct((2 * PEERS, SLOT, 128), bf16)),
        in_specs=[V, pl.BlockSpec(memory_space=pl.ANY), V], out_specs=(V, V),
        scratch_shapes=[pltpu.VMEM((EP_DEV, CELLS, EP_LEN, CIN), bf16), pltpu.VMEM((PEERS, 8, 128), jnp.int32),
                        pltpu.VMEM((PEERS * RANKS * SLOT, 128), f32), pltpu.VMEM((PEERS, SLOT, 128), bf16),
                        pltpu.VMEM((PEERS, SLOT, 128), bf16), pltpu.SemaphoreType.DMA,
                        pltpu.SemaphoreType.DMA((PEERS,)), pltpu.SemaphoreType.DMA((PEERS,)),
                        pltpu.SemaphoreType.DMA((PEERS,)), pltpu.SemaphoreType.DMA((PEERS,))],
        compiler_params=pltpu.CompilerParams(vmem_limit_bytes=56 * 2**20, collective_id=2, has_side_effects=True),
        name="fetch_frames",
    )(asks, replay.transpose(0, 2, 1, 3), instructions)


def vpu_block(lane, tile_pre, tile_sc, dw_ref, F, S1, M, sec, prec, gk_ref):
    ln = pl.ds(lane, 128)
    row = lambda c: slice(c * 8, c * 8 + 8)
    for c in range(CELLS):
        h = tile_pre[row(c), ln]
        t = jnp.tanh(h)
        u = 1.0 + t
        F[row(c), :] = h * u
        S1[row(c), :] = u * (1.0 + h * (1.0 - t))
    taps = [dw_ref[t * 8:t * 8 + 8, ln] for t in range(9)]
    acc = [gk_ref[t * 8:t * 8 + 8, ln] for t in range(9)]
    get = lambda ref, i: [ref[row(i * 9 + k), :] for k in range(9)]
    prev, cur, nxt = None, None, get(F, 0)
    for i in range(9):
        prev, cur = cur, nxt
        nxt = get(F, i + 1) if i < 8 else None
        rows3 = (prev, cur, nxt)
        for k in range(9):
            total = None
            for r in range(3):
                if rows3[r] is None:
                    continue
                for c in range(3):
                    kk = k + c - 1
                    if 0 <= kk < 9:
                        term = taps[3 * r + c] * rows3[r][kk]
                        total = term if total is None else total + term
            h = total
            t = jnp.tanh(h)
            u = 1.0 + t
            sec[row(i * 9 + k), ln] = h * u
            mc = tile_sc[row(i * 9 + k), ln] * (u * (1.0 + h * (1.0 - t)))
            M[row(i * 9 + k), :] = mc
            for r in range(3):
                if rows3[r] is None:
                    continue
                for c in range(3):
                    kk = k + c - 1
                    if 0 <= kk < 9:
                        acc[3 * r + c] = acc[3 * r + c] + mc * rows3[r][kk]
    for t in range(9):
        gk_ref[t * 8:t * 8 + 8, ln] = acc[t]
    prev, cur, nxt = None, None, get(M, 0)
    for i in range(9):
        prev, cur = cur, nxt
        nxt = get(M, i + 1) if i < 8 else None
        rows3 = (nxt, cur, prev)
        for k in range(9):
            total = None
            for r in range(3):
                if rows3[r] is None:
                    continue
                for c in range(3):
                    kk = k - c + 1
                    if 0 <= kk < 9:
                        term = taps[3 * r + c] * rows3[r][kk]
                        total = term if total is None else total + term
            prec[row(i * 9 + k), ln] = total * S1[row(i * 9 + k), :]


def sort_frames(own_ref, named, rank, order):
    def clear(p, c):
        named[p] = 0
        return c
    lax.fori_loop(0, PEERS, clear, 0)

    def note(j, counts):
        o = own_ref[j]
        r = named[o]
        named[o] = r + 1
        rank[j] = r
        return (counts[0] + (r == 0).astype(jnp.int32), counts[1] + (r == 1).astype(jnp.int32))
    n0, n1 = lax.fori_loop(0, FR, note, (jnp.int32(0), jnp.int32(0)))

    def place_frame(j, at):
        r = rank[j]
        p = jnp.where(r == 0, at[0], jnp.where(r == 1, at[1], at[2]))
        order[p] = j
        return tuple(a + (r == k).astype(jnp.int32) for k, a in enumerate(at))
    lax.fori_loop(0, FR, place_frame, (jnp.int32(0), n0, n0 + n1))
    return n0


def block_kernel(last, *refs):
    if last:
        (own_ref, got_ref, more_ref, g_ref, we_ref, dw_ref, wp_ref, wpt_ref, fw_ref, ge0, gpt0, gk0, fc0, e0, tok0,
         tok_ref, sum_ref, *scratch) = refs
        (named, rank, order, x32, xb, g32, pc, e32, pre, sc, sec, prec, secb, precb, proj, F, S1, M,
         ge, gpt, gk, fc, em) = scratch
        fc[...] = fc0[...]
        em[...] = e0[...]
        tok_ref[...] = tok0[...]
    else:
        (own_ref, got_ref, g_ref, we_ref, dw_ref, wp_ref, wpt_ref, fw_ref,
         ge, gpt, gk, fc, em, tok_ref, *scratch) = refs
        (named, rank, order, x32, xb, g32, pc, e32, pre, sc, sec, prec, secb, precb, proj, F, S1, M) = scratch
    for ref in (gk, ge, gpt):
        ref[...] = jnp.zeros_like(ref)
    early = sort_frames(own_ref, named, rank, order) // TILE
    first, stop = (early, NT) if last else (0, early)

    def tile(ft, carry):
        for f in range(TILE):
            p = ft * TILE + f
            keep = jnp.where(p < FR, 1.0, 0.0)
            j = order[jnp.minimum(p, FR - 1)]
            held = got_ref[own_ref[j]]
            if last:
                later = more_ref[own_ref[j] * 2 + jnp.maximum(rank[j], 1) - 1]
                held = jnp.where(rank[j] == 0, held, later)
            held = held.astype(f32) * keep
            for l in range(2):
                x32[l, pl.ds(f, CELLS, stride=TILE), :] = held[l * CELLS:l * CELLS + CELLS]
            for q in range(4):
                e32[f:f + 1, q * 128:q * 128 + 128] = held[2 * CELLS + q:2 * CELLS + q + 1]
            for l in range(3):
                g32[l, pl.ds(f, CELLS, stride=TILE), :] = g_ref[j, :, l * 128:l * 128 + 128].astype(f32) * keep
        for l in range(2):
            xb[:, l * 128:l * 128 + 128] = x32[l].astype(bf16)
        eb = e32[...].astype(bf16)
        em[ft] = eb
        fm = jnp.dot(eb, fw_ref[...], preferred_element_type=f32)
        scale, shift = 1.0 + fm[:, :COUT], fm[:, COUT:]
        for l in range(3):
            sl = slice(l * 128, l * 128 + 128)
            pc[:, sl] = (g32[l].reshape(CELLS, TILE, 128) * scale[None, :, sl]).reshape(ROWS, 128).astype(bf16)
        pre[...] = jnp.dot(xb[...], we_ref[...], preferred_element_type=f32)
        sc[...] = jnp.dot(pc[...], wpt_ref[...], preferred_element_type=f32)

        def lanes(lt, carry):
            vpu_block(pl.multiple_of(lt * 128, 128), pre, sc, dw_ref, F, S1, M, sec, prec, gk)
            return carry
        lax.fori_loop(0, HP // 128, lanes, 0)
        secb[...] = sec[...].astype(bf16)
        precb[...] = prec[...].astype(bf16)
        pj = jnp.dot(secb[...], wp_ref[...], preferred_element_type=f32)
        for l in range(3):
            sl = slice(l * 128, l * 128 + 128)
            g3, pj3 = g32[l].reshape(CELLS, TILE, 128), pj[:, sl].reshape(CELLS, TILE, 128)
            fc[ft, :, sl] = jnp.sum(g3 * pj3, axis=0)
            fc[ft, :, COUT + l * 128:COUT + l * 128 + 128] = jnp.sum(g3, axis=0)
            proj[l] = (pj3 * scale[None, :, sl] + shift[None, :, sl]).reshape(ROWS, 128)
        for f in range(TILE):
            @pl.when(ft * TILE + f < FR)
            def _(f=f):
                j = order[jnp.minimum(ft * TILE + f, FR - 1)]
                for l in range(3):
                    tok_ref[j, :, l * 128:l * 128 + 128] = proj[l, pl.ds(f, CELLS, stride=TILE), :].astype(bf16)
        tn = (((0,), (0,)), ((), ()))
        ge[...] += lax.dot_general(xb[...], precb[...], tn, preferred_element_type=f32)
        gpt[...] += lax.dot_general(pc[...], secb[...], tn, preferred_element_type=f32)
        return carry
    lax.fori_loop(first, stop, tile, 0)
    if not last:
        return
    kernel_sum = jnp.sum((gk[...] + gk0[...]).reshape(9, 8, HP), axis=1)
    kernel_sum = jnp.concatenate([kernel_sum, jnp.zeros((7, HP), f32)], axis=0).astype(bf16)
    for lt in range(HP // 128):
        ln = slice(lt * 128, lt * 128 + 128)
        sum_ref[GE + lt * 240:GE + lt * 240 + 240, :] = (ge[:240, ln] + ge0[:240, ln]).astype(bf16)
        sum_ref[GK + lt * 16:GK + lt * 16 + 16, :] = kernel_sum[:, ln]
    for l in range(3):
        rows = slice(l * 128, l * 128 + 128)
        sum_ref[GP + l * HID:GP + l * HID + HID, :] = (gpt[rows, :] + gpt0[rows, :]).T[:HID].astype(bf16)
    words = em[...].astype(f32).reshape(NT * TILE, EMB).astype(bf16)
    cots = fc[...].reshape(NT * TILE, 2 * COUT).astype(bf16)
    gf = lax.dot_general(words, cots, (((0,), (0,)), ((), ())), preferred_element_type=f32).astype(bf16)
    for l in range(6):
        sum_ref[GF + l * EMB:GF + l * EMB + EMB, :] = gf[:, l * 128:l * 128 + 128]
    sum_ref[GF + 6 * EMB:, :] = jnp.zeros((GR - GF - 6 * EMB, 128), bf16)


def block(last, owner, arrays, state):
    V = pl.BlockSpec(memory_space=pltpu.VMEM)
    S = lambda *shape, t=f32: pltpu.VMEM(shape, t)
    I = lambda n: pltpu.SMEM((n,), jnp.int32)
    O = jax.ShapeDtypeStruct
    held = [((256, HP), f32), ((COUT, HP), f32), ((72, HP), f32), ((NT, TILE, 2 * COUT), f32), ((NT, TILE, EMB), bf16)]
    tok = O((FR, CELLS, COUT), bf16)
    out_shape = (tok, O((GR, 128), bf16)) if last else tuple(O(*h) for h in held) + (tok,)
    scratch = [I(PEERS), I(FR), I(FR), S(2, ROWS, 128), S(ROWS, 256, t=bf16), S(3, ROWS, 128), S(ROWS, COUT, t=bf16), S(TILE, EMB),
               S(ROWS, HP), S(ROWS, HP), S(ROWS, HP), S(ROWS, HP), S(ROWS, HP, t=bf16), S(ROWS, HP, t=bf16), S(3, ROWS, 128),
               S(ROWS, 128), S(ROWS, 128), S(ROWS, 128)]
    if last:
        scratch += [S(*shape, t=kind) for shape, kind in held]
    return pl.pallas_call(
        functools.partial(block_kernel, last),
        out_shape=out_shape,
        in_specs=[pl.BlockSpec(memory_space=pltpu.SMEM)] + [V] * (len(arrays) + len(state)), out_specs=(V,) * len(out_shape),
        scratch_shapes=scratch,
        compiler_params=pltpu.CompilerParams(vmem_limit_bytes=60 * 2**20),
        cost_estimate=pl.CostEstimate(flops=2 * 10**10, bytes_accessed=2 * 10**8, transcendentals=8 * 10**6),
        name="late_frames" if last else "early_frames",
    )(owner, *arrays, *state)


PIECES = (32, 32, 16)
STARTS = (0, 4096, 8192)
ORDERS = (("x", "y", "z"), ("y", "z", "x"), ("z", "x", "y"))


def place():
    dp, rep = lax.axis_index("dp"), lax.axis_index("replica")
    return {"x": rep, "y": dp // 8, "z": (dp // 2) % 4, "core": dp % 2}


def device_of(at):
    return ((at["y"] * 4 + at["z"]) * 2 + at["core"], at["x"])


def shifted(at, axis, d):
    size = 2 if axis == "core" else 4
    other = dict(at)
    other[axis] = (at[axis] + d) % size
    return other


def reduce_kernel(g_ref, ge_ref, gk_ref, gp_ref, gf_ref, total, part, r0, r1, r2, r3, send, recv):
    at = place()
    barrier = pltpu.get_barrier_semaphore()
    peers = [shifted(at, "core", 1)] + [shifted(at, a, d) for a in "xyz" for d in (1, 2, 3)]
    for p in peers:
        pl.semaphore_signal(barrier, inc=1, device_id=device_of(p), device_id_type=pl.DeviceIdType.MESH)
    pl.semaphore_wait(barrier, len(peers))
    land = (r0, r1, r2, r3)
    waits = []

    def push(src, dst, stage, s, d, peer):
        copy = pltpu.make_async_remote_copy(src_ref=src, dst_ref=dst, send_sem=send.at[stage, s, d], recv_sem=recv.at[stage, s, d],
                                            device_id=device_of(peer), device_id_type=pl.DeviceIdType.MESH)
        copy.start()
        waits.append(copy)
        return copy

    def span(base, index, rows):
        return pl.ds(pl.multiple_of(base + index * rows, 16), rows)

    state = []
    for s, r in enumerate(PIECES):
        base, half = STARTS[s], 64 * r
        peer = shifted(at, "core", 1)
        c = push(g_ref.at[span(base, peer["core"], half)], r0.at[pl.ds(base // 2, half)], 0, s, 0, peer)
        state.append([c])
    for stage in (1, 2, 3):
        for s, r in enumerate(PIECES):
            axis = ORDERS[s][stage - 1]
            have = r * 4 ** (4 - stage)
            base = STARTS[s] // 2
            for c in state[s]:
                c.wait_recv()
            if stage == 1:
                mine = g_ref[span(STARTS[s], at["core"], have)].astype(f32) + r0[pl.ds(base, have)].astype(f32)
            else:
                prev = land[stage - 1]
                pb = base // 4 ** (stage - 1)
                old = part[stage - 2, span(base, at[ORDERS[s][stage - 2]], have)].astype(f32)
                mine = old
                for d in (1, 2, 3):
                    mine = mine + prev[d - 1, pl.ds(pb, have)].astype(f32)
            part[stage - 1, pl.ds(base, have)] = mine.astype(bf16)
            block = have // 4
            state[s] = []
            for d in (1, 2, 3):
                peer = shifted(at, axis, d)
                state[s].append(push(part.at[stage - 1, span(base, peer[axis], block)],
                                     land[stage].at[d - 1, pl.ds(base // 4 ** stage, block)], stage, s, d - 1, peer))
    where = []
    for s, r in enumerate(PIECES):
        for c in state[s]:
            c.wait_recv()
        base = STARTS[s] // 2
        mine = part[2, span(base, at[ORDERS[s][2]], r)].astype(f32)
        for d in (1, 2, 3):
            mine = mine + r3[d - 1, pl.ds(base // 64, r)].astype(f32)
        a1, a2, a3 = ORDERS[s]
        index = ((at["core"] * 4 + at[a1]) * 4 + at[a2]) * 4 + at[a3]
        where.append(index)
        total[span(STARTS[s], index, r)] = mine.astype(bf16)
        state[s] = []
        for d in (1, 2, 3):
            sl = span(STARTS[s], index, r)
            state[s].append(push(total.at[sl], total.at[sl], 4, s, d - 1, shifted(at, a3, d)))
    for stage in (5, 6, 7):
        for s, r in enumerate(PIECES):
            for c in state[s]:
                c.wait_recv()
            rows = r * 4 ** (stage - 4)
            index = where[s] // 4 ** (stage - 4)
            sl = span(STARTS[s], index, rows)
            state[s] = []
            if stage == 7:
                state[s].append(push(total.at[sl], total.at[sl], stage, s, 0, shifted(at, "core", 1)))
            else:
                axis = ORDERS[s][6 - stage]
                for d in (1, 2, 3):
                    state[s].append(push(total.at[sl], total.at[sl], stage, s, d - 1, shifted(at, axis, d)))
    for s in range(3):
        for c in state[s]:
            c.wait_recv()
    for c in waits:
        c.wait_send()
    for lt in range(11):
        w = min(128, HID - lt * 128)
        ge_ref[:, lt * 128:lt * 128 + w] = total[GE + lt * 240:GE + lt * 240 + 240].astype(f32)[:CIN, :w]
        gk_ref[:, lt * 128:lt * 128 + w] = total[GK + lt * 16:GK + lt * 16 + 16].astype(f32)[:9, :w]
    for l in range(3):
        gp_ref[:, l * 128:l * 128 + 128] = total[GP + l * HID:GP + l * HID + HID].astype(f32)
    for l in range(6):
        gf_ref[:, l * 128:l * 128 + 128] = total[GF + l * EMB:GF + l * EMB + EMB].astype(f32)


def all_reduce(g):
    V = pl.BlockSpec(memory_space=pltpu.VMEM)
    return pl.pallas_call(
        reduce_kernel,
        out_shape=(jax.ShapeDtypeStruct((CIN, HID), f32), jax.ShapeDtypeStruct((9, HID), f32),
                   jax.ShapeDtypeStruct((HID, COUT), f32), jax.ShapeDtypeStruct((EMB, 2 * COUT), f32)),
        in_specs=[V], out_specs=(V,) * 4,
        scratch_shapes=[pltpu.VMEM((GR, 128), bf16), pltpu.VMEM((3, GR // 2, 128), bf16), pltpu.VMEM((GR // 2, 128), bf16),
                        pltpu.VMEM((3, GR // 8, 128), bf16), pltpu.VMEM((3, GR // 32, 128), bf16), pltpu.VMEM((3, GR // 128, 128), bf16),
                        pltpu.SemaphoreType.DMA((8, 3, 3)), pltpu.SemaphoreType.DMA((8, 3, 3))],
        compiler_params=pltpu.CompilerParams(vmem_limit_bytes=48 * 2**20, collective_id=1, has_side_effects=True),
        name="grad_sum",
    )(g)


def per_device(replay, instructions, owners, episode_rows, frame_steps, w_expand, dw_kernel, w_project, film_weight, token_grad):
    owner = owners[:, 0]
    asks = jnp.stack([jnp.pad(owner, (0, 128 - FR), constant_values=-1), jnp.pad(episode_rows * EP_LEN + frame_steps, (0, 128 - FR))])
    asks = jnp.pad(asks, ((0, 6), (0, 0)))
    got, later = fetch(asks, replay, instructions)
    more = lax.all_to_all(later.reshape(PEERS, 2, SLOT, 128), "dp", split_axis=0, concat_axis=0, tiled=True).reshape(2 * PEERS, SLOT, 128)
    g = token_grad.reshape(FR, CELLS, COUT)
    we = jnp.pad(w_expand * jnp.asarray(0.5, bf16), ((0, 256 - CIN), (0, HP - HID)))
    wp = jnp.pad(w_project, ((0, HP - HID), (0, 0)))
    wpt = jnp.pad((w_project * jnp.asarray(0.5, bf16)).T, ((0, 0), (0, HP - HID)))
    dw = jnp.repeat(jnp.pad(dw_kernel * 0.5, ((0, 0), (0, HP - HID))), 8, axis=0)
    weights = (g, we, dw, wp, wpt, film_weight)
    state = block(False, owner, (got,) + weights, ())
    tokens, partial_sums = block(True, owner, (got, more) + weights, state)
    return (tokens.reshape(token_grad.shape), *all_reduce(partial_sums))


def solution(mesh):
    split = ("dp", "replica")
    in_specs = (P(split), P(split), P(split), P(split), P(split), P(), P(), P(), P(), P(split))
    return jax.shard_map(per_device, mesh=mesh, in_specs=in_specs, out_specs=(P(split), P(), P(), P(), P()), check_vma=False)
```

```python
import functools
import jax, jax.numpy as jnp
from jax import lax
from jax.experimental import pallas as pl
from jax.experimental.pallas import tpu as pltpu
from jax.sharding import PartitionSpec as P

SIDE, CELLS, TILE = 9, 81, 8
CIN, HID, COUT, EMB, FR = 232, 1392, 384, 512, 36
HP = 1408
NL = HP // 128
NT = 5
ROWS = CELLS * TILE
PEERS, RANKS, SLOT = 32, 3, 176
EP_DEV, EP_LEN = 8, 24
GR = 10240
GE, GK, GP, GF = 0, 2640, 2816, 6992
f32, bf16 = jnp.float32, jnp.bfloat16


def fetch_kernel(own_ref, row_ref, step_ref, rep_ref, ins_ref, got_ref, later_ref,
                 rep, ask_ref, asks, stage, out, got, rep_sem, ask_send, ask_recv, send, recv):
    me, rail = lax.axis_index("dp"), lax.axis_index("replica")
    load = pltpu.make_async_copy(rep_ref, rep, rep_sem)
    load.start()
    ask_ref[...] = jnp.full((8, 128), -1, jnp.int32)
    ask_ref[0:1, :FR] = own_ref[...]
    ask_ref[1:2, :FR] = row_ref[...] * EP_LEN + step_ref[...]
    barrier = pltpu.get_barrier_semaphore()

    def peer(d):
        return lax.rem(me + d, PEERS)

    def greet(d, c):
        pl.semaphore_signal(barrier, inc=1, device_id=(peer(d), rail), device_id_type=pl.DeviceIdType.MESH)
        return c
    lax.fori_loop(1, PEERS, greet, 0)
    pl.semaphore_wait(barrier, PEERS - 1)

    def ask(d):
        return pltpu.make_async_remote_copy(src_ref=ask_ref, dst_ref=asks.at[me], send_sem=ask_send.at[d], recv_sem=ask_recv.at[d],
                                            device_id=(peer(d), rail), device_id_type=pl.DeviceIdType.MESH)

    def frame(d):
        return pltpu.make_async_remote_copy(src_ref=out.at[peer(d)], dst_ref=got.at[me], send_sem=send.at[d], recv_sem=recv.at[d],
                                            device_id=(peer(d), rail), device_id_type=pl.DeviceIdType.MESH)

    def each(f):
        def body(d, c):
            f(d)
            return c
        lax.fori_loop(1, PEERS, body, 0)
    each(lambda d: ask(d).start())
    asks[me] = ask_ref[...]
    zero = jnp.zeros((PEERS * RANKS, 128), f32)
    for r in range(2 * CELLS + 4, SLOT):
        stage[pl.ds(r, PEERS * RANKS, stride=SLOT), :] = zero
    each(lambda d: ask(d).wait_recv())
    owner, wanted = asks[:, 0, :], asks[:, 1, :]
    mine = owner == me
    before = lax.broadcasted_iota(jnp.int32, (128, 128), 0) < lax.broadcasted_iota(jnp.int32, (128, 128), 1)
    rank = jnp.dot(jnp.where(mine, 1.0, 0.0).astype(bf16), jnp.where(before, 1.0, 0.0).astype(bf16), preferred_element_type=f32)
    wide = wanted.astype(f32)
    picks = []
    for k in range(RANKS):
        hit = mine & (rank > k - 0.5) & (rank < k + 0.5)
        picks.append(jnp.sum(jnp.where(hit, wide + 1.0, 0.0), axis=1, keepdims=True) - 1.0)
    pick = jnp.concatenate(picks, axis=0)
    at = lax.broadcasted_iota(jnp.int32, (PEERS * RANKS, EP_DEV * EP_LEN), 1).astype(f32)
    choose = jnp.where(pick == at, 1.0, 0.0).astype(bf16)
    low = lax.broadcasted_iota(jnp.int32, (PEERS * RANKS, EP_DEV), 1).astype(f32) * EP_LEN
    which = jnp.where((pick >= low) & (pick < low + EP_LEN), 1.0, 0.0).astype(bf16)
    words = jnp.dot(which, ins_ref[...], preferred_element_type=f32)

    def put(row, values):
        stage[pl.ds(row, PEERS, stride=SLOT), :] = values[:PEERS]

    def put_later(row, values):
        for k in range(2):
            stage[pl.ds((PEERS + k) * SLOT + row, PEERS, stride=2 * SLOT), :] = values[k * PEERS:k * PEERS + PEERS]
    for q in range(4):
        put(2 * CELLS + q, words[:PEERS, q * 128:q * 128 + 128])
        put_later(2 * CELLS + q, words[PEERS:, q * 128:q * 128 + 128])
    load.wait()

    def cells(chosen, store):
        blank = jnp.zeros((chosen.shape[0], 256 - CIN), f32)

        def some(i, carry):
            for u in range(3):
                c = i * 3 + u
                found = jnp.dot(chosen, rep[:, c].reshape(EP_DEV * EP_LEN, CIN), preferred_element_type=f32)
                store(c, found[:, :128])
                store(CELLS + c, jnp.concatenate([found[:, 128:], blank], axis=1))
            return carry
        lax.fori_loop(0, CELLS // 3, some, 0)
    cells(choose[:PEERS], put)

    def pack(p, carry):
        out[p] = stage[pl.ds(pl.multiple_of(p * SLOT, 8), SLOT), :].astype(bf16)
        return carry
    lax.fori_loop(0, PEERS, pack, 0)
    each(lambda d: frame(d).start())
    got[me] = out[me]
    cells(choose[PEERS:], put_later)

    def pack_later(p, carry):
        later_ref[p] = stage[pl.ds(pl.multiple_of((PEERS + p) * SLOT, 8), SLOT), :].astype(bf16)
        return carry
    lax.fori_loop(0, 2 * PEERS, pack_later, 0)
    each(lambda d: ask(d).wait_send())
    each(lambda d: frame(d).wait_recv())
    got_ref[...] = got[...]
    each(lambda d: frame(d).wait_send())


def fetch(owner, row, step, replay, instructions):
    V = pl.BlockSpec(memory_space=pltpu.VMEM)
    return pl.pallas_call(
        fetch_kernel,
        out_shape=(jax.ShapeDtypeStruct((PEERS, SLOT, 128), bf16), jax.ShapeDtypeStruct((2 * PEERS, SLOT, 128), bf16)),
        in_specs=[V, V, V, pl.BlockSpec(memory_space=pl.ANY), V], out_specs=(V, V),
        scratch_shapes=[pltpu.VMEM((EP_DEV, CELLS, EP_LEN, CIN), bf16), pltpu.VMEM((8, 128), jnp.int32), pltpu.VMEM((PEERS, 8, 128), jnp.int32),
                        pltpu.VMEM((PEERS * RANKS * SLOT, 128), f32), pltpu.VMEM((PEERS, SLOT, 128), bf16),
                        pltpu.VMEM((PEERS, SLOT, 128), bf16), pltpu.SemaphoreType.DMA,
                        pltpu.SemaphoreType.DMA((PEERS,)), pltpu.SemaphoreType.DMA((PEERS,)),
                        pltpu.SemaphoreType.DMA((PEERS,)), pltpu.SemaphoreType.DMA((PEERS,))],
        compiler_params=pltpu.CompilerParams(vmem_limit_bytes=56 * 2**20, collective_id=2, has_side_effects=True),
        name="fetch_frames",
    )(owner, row, step, replay.transpose(0, 2, 1, 3), instructions)


def vpu_block(pre, sc, dw_ref, F, S1, M, sec, prec, gk_ref):
    row = lambda c: slice(c * 8, c * 8 + 8)
    tap = lambda t: dw_ref[t * 8:t * 8 + 8, :]
    acc = [gk_ref[t * 8:t * 8 + 8, :] for t in range(9)]
    get = lambda ref, i: [ref[row(i * 9 + k), :] for k in range(9)] if 0 <= i < 9 else None

    def activate(i):
        for k in range(9):
            c = i * 9 + k
            h = pre[row(c), :]
            t = jnp.tanh(h)
            u = 1.0 + t
            F[row(c), :] = (h * u).astype(bf16).astype(f32)
            S1[row(c), :] = u * (1.0 + h * (1.0 - t))

    def ahead(i):
        rows3 = (get(F, i - 1), get(F, i), get(F, i + 1))
        for k in range(9):
            near = [(3 * r + c, rows3[r][k + c - 1]) for r in range(3) if rows3[r] for c in range(3) if 0 <= k + c - 1 < 9]
            h = None
            for t, v in near:
                h = tap(t) * v if h is None else h + tap(t) * v
            t = jnp.tanh(h)
            u = 1.0 + t
            sec[row(i * 9 + k), :] = h * u
            mc = sc[row(i * 9 + k), :] * (u * (1.0 + h * (1.0 - t)))
            M[row(i * 9 + k), :] = mc
            for t, v in near:
                acc[t] = acc[t] + mc * v

    def back(i):
        rows3 = (get(M, i + 1), get(M, i), get(M, i - 1))
        for k in range(9):
            total = None
            for r in range(3):
                for c in range(3):
                    if rows3[r] and 0 <= k - c + 1 < 9:
                        term = tap(3 * r + c) * rows3[r][k - c + 1]
                        total = term if total is None else total + term
            prec[row(i * 9 + k), :] = total * S1[row(i * 9 + k), :]
    for i in range(9):
        activate(i)
    for i in range(9):
        ahead(i)
    for i in range(9):
        back(i)
    for t in range(9):
        gk_ref[t * 8:t * 8 + 8, :] = acc[t]


def sort_frames(own_ref, named, rank, order):
    def clear(p, c):
        named[p] = 0
        return c
    lax.fori_loop(0, PEERS, clear, 0)

    def note(j, counts):
        o = own_ref[j]
        r = named[o]
        named[o] = r + 1
        rank[j] = r
        return (counts[0] + (r == 0).astype(jnp.int32), counts[1] + (r == 1).astype(jnp.int32))
    n0, n1 = lax.fori_loop(0, FR, note, (jnp.int32(0), jnp.int32(0)))

    def place_frame(j, at):
        r = rank[j]
        p = jnp.where(r == 0, at[0], jnp.where(r == 1, at[1], at[2]))
        order[p] = j
        return tuple(a + (r == k).astype(jnp.int32) for k, a in enumerate(at))
    lax.fori_loop(0, FR, place_frame, (jnp.int32(0), n0, n0 + n1))
    return n0


def prepare(wx_ref, kern_ref, wj_ref, we, dw, wp, wpt):
    we[...] = jnp.zeros_like(we)
    we[:CIN, :HID] = wx_ref[...] * jnp.asarray(0.5, bf16)
    wp[:HID, :] = wj_ref[...]
    wp[HID:, :] = jnp.zeros((HP - HID, COUT), bf16)
    wpt[...] = wp[...].T * jnp.asarray(0.5, bf16)
    taps = jnp.concatenate([kern_ref[...] * 0.5, jnp.zeros((9, HP - HID), f32)], axis=1)
    for k in range(NL):
        for t in range(9):
            dw[k, t * 8:t * 8 + 8, :] = jnp.broadcast_to(taps[t:t + 1, k * 128:k * 128 + 128], (8, 128))


def block_kernel(last, *refs):
    if last:
        (own_ref, got_ref, g_ref, fw_ref, more_ref, we_ref, dw_ref, wp_ref, wpt_ref, fc0, e0, ge0, gpt0, gk0, tok0,
         tok_ref, sum_ref, *scratch) = refs
        (named, rank, order, x32, xb, g32, pc, e32, pre, sc, sec, prec, secb, precb, proj, F, S1, M, tokens, tok_sem,
         ge, gpt, gk, fc, em, ge1, gpt1, gk1, sums_sem) = scratch
        loads = [pltpu.make_async_copy(src, dst, sums_sem.at[n]) for n, (src, dst) in enumerate(((ge0, ge1), (gpt0, gpt1), (gk0, gk1)))]
        for load in loads:
            load.start()
        fc[...] = fc0[...]
        em[...] = e0[...]
    else:
        (own_ref, got_ref, g_ref, fw_ref, wx_ref, kern_ref, wj_ref,
         we_ref, dw_ref, wp_ref, wpt_ref, fc, em, ge, gpt, gk, tok_ref, *scratch) = refs
        (named, rank, order, x32, xb, g32, pc, e32, pre, sc, sec, prec, secb, precb, proj, F, S1, M, tokens, tok_sem) = scratch
        prepare(wx_ref, kern_ref, wj_ref, we_ref, dw_ref, wp_ref, wpt_ref)
    for ref in (gk, ge, gpt):
        ref[...] = jnp.zeros_like(ref)
    early = sort_frames(own_ref, named, rank, order) // TILE
    first, stop = (early, NT) if last else (0, early)

    def tile(ft, carry):
        for f in range(TILE):
            p = ft * TILE + f
            keep = jnp.where(p < FR, 1.0, 0.0)
            j = order[jnp.minimum(p, FR - 1)]
            held = got_ref[own_ref[j]]
            if last:
                later = more_ref[own_ref[j] * 2 + jnp.maximum(rank[j], 1) - 1]
                held = jnp.where(rank[j] == 0, held, later)
            held = held.astype(f32) * keep
            for l in range(2):
                x32[l, pl.ds(f, CELLS, stride=TILE), :] = held[l * CELLS:l * CELLS + CELLS]
            for q in range(4):
                e32[f:f + 1, q * 128:q * 128 + 128] = held[2 * CELLS + q:2 * CELLS + q + 1]
            for l in range(3):
                g32[l, pl.ds(f, CELLS, stride=TILE), :] = g_ref[j, :, l * 128:l * 128 + 128].astype(f32) * keep
        for l in range(2):
            xb[:, l * 128:l * 128 + 128] = x32[l].astype(bf16)
        eb = e32[...].astype(bf16)
        em[ft] = eb
        fm = jnp.dot(eb, fw_ref[...], preferred_element_type=f32)
        scale, shift = 1.0 + fm[:, :COUT], fm[:, COUT:]
        for l in range(3):
            sl = slice(l * 128, l * 128 + 128)
            pc[:, sl] = (g32[l].reshape(CELLS, TILE, 128) * scale[None, :, sl]).reshape(ROWS, 128).astype(bf16)
        hidden = jnp.dot(xb[...], we_ref[...], preferred_element_type=f32)
        for k in range(NL):
            pre[k] = hidden[:, k * 128:k * 128 + 128]
        hidden = jnp.dot(pc[...], wpt_ref[...], preferred_element_type=f32)
        for k in range(NL):
            sc[k] = hidden[:, k * 128:k * 128 + 128]

        def one(k, n):
            vpu_block(pre.at[k], sc.at[k], dw_ref.at[k], F.at[n], S1.at[n], M.at[n], sec.at[k], prec.at[k], gk.at[k])

        def lanes(i, carry):
            one(2 * i, 0)
            one(2 * i + 1, 1)
            return carry
        lax.fori_loop(0, NL // 2, lanes, 0)
        one(NL - 1, 0)
        for k in range(NL):
            secb[:, k * 128:k * 128 + 128] = sec[k].astype(bf16)
            precb[:, k * 128:k * 128 + 128] = prec[k].astype(bf16)
        pj = jnp.dot(secb[...], wp_ref[...], preferred_element_type=f32)
        for l in range(3):
            sl = slice(l * 128, l * 128 + 128)
            g3, pj3 = g32[l].reshape(CELLS, TILE, 128), pj[:, sl].reshape(CELLS, TILE, 128)
            fc[ft, :, sl] = jnp.sum(g3 * pj3, axis=0)
            fc[ft, :, COUT + l * 128:COUT + l * 128 + 128] = jnp.sum(g3, axis=0)
            proj[l] = (pj3 * scale[None, :, sl] + shift[None, :, sl]).reshape(ROWS, 128)
        def token_copy(f):
            j = order[jnp.minimum(ft * TILE + f, FR - 1)]
            return pltpu.make_async_copy(tokens.at[f], tok_ref.at[j], tok_sem.at[f])
        for f in range(TILE):
            for l in range(3):
                tokens[f, :, l * 128:l * 128 + 128] = proj[l, pl.ds(f, CELLS, stride=TILE), :].astype(bf16)

            @pl.when(ft * TILE + f < FR)
            def _(f=f):
                token_copy(f).start()
        tn = (((0,), (0,)), ((), ()))
        ge[...] += lax.dot_general(xb[...], precb[...], tn, preferred_element_type=f32)
        gpt[...] += lax.dot_general(pc[...], secb[...], tn, preferred_element_type=f32)
        for f in range(TILE):
            @pl.when(ft * TILE + f < FR)
            def _(f=f):
                token_copy(f).wait()
        return carry
    lax.fori_loop(first, stop, tile, 0)
    if not last:
        return
    for load in loads:
        load.wait()
    for k in range(NL):
        ln = slice(k * 128, k * 128 + 128)
        sum_ref[GE + k * 240:GE + k * 240 + 240, :] = (ge[:240, ln] + ge1[:240, ln]).astype(bf16)
        taps = jnp.sum((gk[k] + gk1[k]).reshape(9, 8, 128), axis=1)
        sum_ref[GK + k * 16:GK + k * 16 + 16, :] = jnp.concatenate([taps, jnp.zeros((7, 128), f32)], axis=0).astype(bf16)
    for l in range(3):
        rows = slice(l * 128, l * 128 + 128)
        sum_ref[GP + l * HID:GP + l * HID + HID, :] = (gpt[rows, :] + gpt1[rows, :]).T[:HID].astype(bf16)
    words = em[...].astype(f32).reshape(NT * TILE, EMB).astype(bf16)
    cots = fc[...].reshape(NT * TILE, 2 * COUT).astype(bf16)
    gf = lax.dot_general(words, cots, (((0,), (0,)), ((), ())), preferred_element_type=f32).astype(bf16)
    for l in range(6):
        sum_ref[GF + l * EMB:GF + l * EMB + EMB, :] = gf[:, l * 128:l * 128 + 128]
    sum_ref[GF + 6 * EMB:, :] = jnp.zeros((GR - GF - 6 * EMB, 128), bf16)


def block(last, owner, arrays):
    V, A = pl.BlockSpec(memory_space=pltpu.VMEM), pl.BlockSpec(memory_space=pl.ANY)
    S = lambda *shape, t=f32: pltpu.VMEM(shape, t)
    I = lambda n: pltpu.SMEM((n,), jnp.int32)
    O = jax.ShapeDtypeStruct
    weights = [((256, HP), bf16), ((NL, 72, 128), f32), ((HP, COUT), bf16), ((COUT, HP), bf16)]
    frames = [((NT, TILE, 2 * COUT), f32), ((NT, TILE, EMB), bf16)]
    sums = [((256, HP), f32), ((COUT, HP), f32), ((NL, 72, 128), f32)]
    tok = O((FR, CELLS, COUT), bf16)
    scratch = [I(PEERS), I(FR), I(FR), S(2, ROWS, 128), S(ROWS, 256, t=bf16), S(3, ROWS, 128), S(ROWS, COUT, t=bf16), S(TILE, EMB),
               S(NL, ROWS, 128), S(NL, ROWS, 128), S(NL, ROWS, 128), S(NL, ROWS, 128), S(ROWS, HP, t=bf16), S(ROWS, HP, t=bf16),
               S(3, ROWS, 128), S(2, ROWS, 128), S(2, ROWS, 128), S(2, ROWS, 128), S(TILE, CELLS, COUT, t=bf16), pltpu.SemaphoreType.DMA((TILE,))]
    smem = pl.BlockSpec(memory_space=pltpu.SMEM)
    if last:
        out_shape, out_specs = (tok, O((GR, 128), bf16)), (A, V)
        in_specs = [smem] + [V] * 10 + [A] * 4
        scratch += [S(*shape, t=kind) for shape, kind in sums + frames + sums] + [pltpu.SemaphoreType.DMA((3,))]
        aliases = {14: 0}
    else:
        out_shape = tuple(O(*h) for h in weights + frames + sums) + (tok,)
        out_specs, in_specs, aliases = (V,) * 9 + (A,), [smem] + [V] * 6, {}
    return pl.pallas_call(
        functools.partial(block_kernel, last),
        out_shape=out_shape, in_specs=in_specs, out_specs=out_specs, scratch_shapes=scratch, input_output_aliases=aliases,
        compiler_params=pltpu.CompilerParams(vmem_limit_bytes=61 * 2**20),
        cost_estimate=pl.CostEstimate(flops=2 * 10**10, bytes_accessed=2 * 10**8, transcendentals=8 * 10**6),
        name="late_frames" if last else "early_frames",
    )(owner, *arrays)


PIECES = (32, 32, 16)
STARTS = (0, 4096, 8192)
ORDERS = (("x", "y", "z"), ("y", "z", "x"), ("z", "x", "y"))


def place():
    dp, rep = lax.axis_index("dp"), lax.axis_index("replica")
    return {"x": rep, "y": dp // 8, "z": (dp // 2) % 4, "core": dp % 2}


def device_of(at):
    return ((at["y"] * 4 + at["z"]) * 2 + at["core"], at["x"])


def shifted(at, axis, d):
    size = 2 if axis == "core" else 4
    other = dict(at)
    other[axis] = (at[axis] + d) % size
    return other


def reduce_kernel(g_ref, ge_ref, gk_ref, gp_ref, gf_ref, total, part, r0, r1, r2, r3, send, recv):
    at = place()
    barrier = pltpu.get_barrier_semaphore()
    peers = [shifted(at, "core", 1)] + [shifted(at, a, d) for a in "xyz" for d in (1, 2, 3)]
    for p in peers:
        pl.semaphore_signal(barrier, inc=1, device_id=device_of(p), device_id_type=pl.DeviceIdType.MESH)
    pl.semaphore_wait(barrier, len(peers))
    land = (r0, r1, r2, r3)
    waits = []

    def push(src, dst, stage, s, d, peer):
        copy = pltpu.make_async_remote_copy(src_ref=src, dst_ref=dst, send_sem=send.at[stage, s, d], recv_sem=recv.at[stage, s, d],
                                            device_id=device_of(peer), device_id_type=pl.DeviceIdType.MESH)
        copy.start()
        waits.append(copy)
        return copy

    def span(base, index, rows):
        return pl.ds(pl.multiple_of(base + index * rows, 16), rows)

    state = []
    for s, r in enumerate(PIECES):
        base, half = STARTS[s], 64 * r
        peer = shifted(at, "core", 1)
        c = push(g_ref.at[span(base, peer["core"], half)], r0.at[pl.ds(base // 2, half)], 0, s, 0, peer)
        state.append([c])
    for stage in (1, 2, 3):
        for s, r in enumerate(PIECES):
            axis = ORDERS[s][stage - 1]
            have = r * 4 ** (4 - stage)
            base = STARTS[s] // 2
            for c in state[s]:
                c.wait_recv()
            if stage == 1:
                mine = g_ref[span(STARTS[s], at["core"], have)].astype(f32) + r0[pl.ds(base, have)].astype(f32)
            else:
                prev = land[stage - 1]
                pb = base // 4 ** (stage - 1)
                old = part[stage - 2, span(base, at[ORDERS[s][stage - 2]], have)].astype(f32)
                mine = old
                for d in (1, 2, 3):
                    mine = mine + prev[d - 1, pl.ds(pb, have)].astype(f32)
            part[stage - 1, pl.ds(base, have)] = mine.astype(bf16)
            block = have // 4
            state[s] = []
            for d in (1, 2, 3):
                peer = shifted(at, axis, d)
                state[s].append(push(part.at[stage - 1, span(base, peer[axis], block)],
                                     land[stage].at[d - 1, pl.ds(base // 4 ** stage, block)], stage, s, d - 1, peer))
    where = []
    for s, r in enumerate(PIECES):
        for c in state[s]:
            c.wait_recv()
        base = STARTS[s] // 2
        mine = part[2, span(base, at[ORDERS[s][2]], r)].astype(f32)
        for d in (1, 2, 3):
            mine = mine + r3[d - 1, pl.ds(base // 64, r)].astype(f32)
        a1, a2, a3 = ORDERS[s]
        index = ((at["core"] * 4 + at[a1]) * 4 + at[a2]) * 4 + at[a3]
        where.append(index)
        total[span(STARTS[s], index, r)] = mine.astype(bf16)
        state[s] = []
        for d in (1, 2, 3):
            sl = span(STARTS[s], index, r)
            state[s].append(push(total.at[sl], total.at[sl], 4, s, d - 1, shifted(at, a3, d)))
    for stage in (5, 6, 7):
        for s, r in enumerate(PIECES):
            for c in state[s]:
                c.wait_recv()
            rows = r * 4 ** (stage - 4)
            index = where[s] // 4 ** (stage - 4)
            sl = span(STARTS[s], index, rows)
            state[s] = []
            if stage == 7:
                state[s].append(push(total.at[sl], total.at[sl], stage, s, 0, shifted(at, "core", 1)))
            else:
                axis = ORDERS[s][6 - stage]
                for d in (1, 2, 3):
                    state[s].append(push(total.at[sl], total.at[sl], stage, s, d - 1, shifted(at, axis, d)))
    for s in range(3):
        for c in state[s]:
            c.wait_recv()
    for c in waits:
        c.wait_send()
    for lt in range(11):
        w = min(128, HID - lt * 128)
        ge_ref[:, lt * 128:lt * 128 + w] = total[GE + lt * 240:GE + lt * 240 + 240].astype(f32)[:CIN, :w]
        gk_ref[:, lt * 128:lt * 128 + w] = total[GK + lt * 16:GK + lt * 16 + 16].astype(f32)[:9, :w]
    for l in range(3):
        gp_ref[:, l * 128:l * 128 + 128] = total[GP + l * HID:GP + l * HID + HID].astype(f32)
    for l in range(6):
        gf_ref[:, l * 128:l * 128 + 128] = total[GF + l * EMB:GF + l * EMB + EMB].astype(f32)


def all_reduce(g):
    V = pl.BlockSpec(memory_space=pltpu.VMEM)
    return pl.pallas_call(
        reduce_kernel,
        out_shape=(jax.ShapeDtypeStruct((CIN, HID), f32), jax.ShapeDtypeStruct((9, HID), f32),
                   jax.ShapeDtypeStruct((HID, COUT), f32), jax.ShapeDtypeStruct((EMB, 2 * COUT), f32)),
        in_specs=[V], out_specs=(V,) * 4,
        scratch_shapes=[pltpu.VMEM((GR, 128), bf16), pltpu.VMEM((3, GR // 2, 128), bf16), pltpu.VMEM((GR // 2, 128), bf16),
                        pltpu.VMEM((3, GR // 8, 128), bf16), pltpu.VMEM((3, GR // 32, 128), bf16), pltpu.VMEM((3, GR // 128, 128), bf16),
                        pltpu.SemaphoreType.DMA((8, 3, 3)), pltpu.SemaphoreType.DMA((8, 3, 3))],
        compiler_params=pltpu.CompilerParams(vmem_limit_bytes=48 * 2**20, collective_id=1, has_side_effects=True),
        name="grad_sum",
    )(g)


def per_device(replay, instructions, owners, episode_rows, frame_steps, w_expand, dw_kernel, w_project, film_weight, token_grad):
    owner = owners[:, 0]
    got, later = fetch(owner.reshape(1, FR), episode_rows.reshape(1, FR), frame_steps.reshape(1, FR), replay, instructions)
    more = lax.all_to_all(later.reshape(PEERS, 2, SLOT, 128), "dp", split_axis=0, concat_axis=0, tiled=True).reshape(2 * PEERS, SLOT, 128)
    g = token_grad.reshape(FR, CELLS, COUT)
    *weights, cots, words, grad_e, grad_p, grad_k, tokens = block(False, owner, (got, g, film_weight, w_expand, dw_kernel, w_project))
    tokens, partial_sums = block(True, owner, (got, g, film_weight, more, *weights, cots, words, grad_e, grad_p, grad_k, tokens))
    return (tokens.reshape(token_grad.shape), *all_reduce(partial_sums))


def solution(mesh):
    split = ("dp", "replica")
    in_specs = (P(split), P(split), P(split), P(split), P(split), P(), P(), P(), P(), P(split))
    return jax.shard_map(per_device, mesh=mesh, in_specs=in_specs, out_specs=(P(split), P(), P(), P(), P()), check_vma=False)
```

```python
import functools
import jax, jax.numpy as jnp
from jax import lax
from jax.experimental import pallas as pl
from jax.experimental.pallas import tpu as pltpu
from jax.sharding import PartitionSpec as P

SIDE, CELLS, TILE = 9, 81, 8
CIN, HID, COUT, EMB, FR = 232, 1392, 384, 512, 36
HP = 1408
NL = HP // 128
NT = 5
ROWS = CELLS * TILE
PEERS, RANKS, SLOT = 32, 3, 176
EP_DEV, EP_LEN = 8, 24
GR = 10240
GE, GK, GP, GF = 0, 2640, 2816, 6992
f32, bf16 = jnp.float32, jnp.bfloat16


def fetch_kernel(own_ref, row_ref, step_ref, rep_ref, ins_ref, got_ref, later_ref,
                 rep, ask_ref, asks, stage, out, got, rep_sem, ask_send, ask_recv, send, recv):
    me, rail = lax.axis_index("dp"), lax.axis_index("replica")
    load = pltpu.make_async_copy(rep_ref, rep, rep_sem)
    load.start()
    ask_ref[...] = jnp.full((8, 128), -1, jnp.int32)
    ask_ref[0:1, :FR] = own_ref[...]
    ask_ref[1:2, :FR] = row_ref[...] * EP_LEN + step_ref[...]
    barrier = pltpu.get_barrier_semaphore()

    def peer(d):
        return lax.rem(me + d, PEERS)

    def greet(d, c):
        pl.semaphore_signal(barrier, inc=1, device_id=(peer(d), rail), device_id_type=pl.DeviceIdType.MESH)
        return c
    lax.fori_loop(1, PEERS, greet, 0)
    pl.semaphore_wait(barrier, PEERS - 1)

    def ask(d):
        return pltpu.make_async_remote_copy(src_ref=ask_ref, dst_ref=asks.at[me], send_sem=ask_send.at[d], recv_sem=ask_recv.at[d],
                                            device_id=(peer(d), rail), device_id_type=pl.DeviceIdType.MESH)

    def frame(d):
        return pltpu.make_async_remote_copy(src_ref=out.at[peer(d)], dst_ref=got.at[me], send_sem=send.at[d], recv_sem=recv.at[d],
                                            device_id=(peer(d), rail), device_id_type=pl.DeviceIdType.MESH)

    def each(f):
        def body(d, c):
            f(d)
            return c
        lax.fori_loop(1, PEERS, body, 0)
    each(lambda d: ask(d).start())
    asks[me] = ask_ref[...]
    zero = jnp.zeros((PEERS * RANKS, 128), f32)
    for r in range(2 * CELLS + 4, SLOT):
        stage[pl.ds(r, PEERS * RANKS, stride=SLOT), :] = zero
    each(lambda d: ask(d).wait_recv())
    owner, wanted = asks[:, 0, :], asks[:, 1, :]
    mine = owner == me
    before = lax.broadcasted_iota(jnp.int32, (128, 128), 0) < lax.broadcasted_iota(jnp.int32, (128, 128), 1)
    rank = jnp.dot(jnp.where(mine, 1.0, 0.0).astype(bf16), jnp.where(before, 1.0, 0.0).astype(bf16), preferred_element_type=f32)
    wide = wanted.astype(f32)
    picks = []
    for k in range(RANKS):
        hit = mine & (rank > k - 0.5) & (rank < k + 0.5)
        picks.append(jnp.sum(jnp.where(hit, wide + 1.0, 0.0), axis=1, keepdims=True) - 1.0)
    pick = jnp.concatenate(picks, axis=0)
    at = lax.broadcasted_iota(jnp.int32, (PEERS * RANKS, EP_DEV * EP_LEN), 1).astype(f32)
    choose = jnp.where(pick == at, 1.0, 0.0).astype(bf16)
    low = lax.broadcasted_iota(jnp.int32, (PEERS * RANKS, EP_DEV), 1).astype(f32) * EP_LEN
    which = jnp.where((pick >= low) & (pick < low + EP_LEN), 1.0, 0.0).astype(bf16)
    words = jnp.dot(which, ins_ref[...], preferred_element_type=f32)

    def put(row, values):
        stage[pl.ds(row, PEERS, stride=SLOT), :] = values[:PEERS]

    def put_later(row, values):
        for k in range(2):
            stage[pl.ds((PEERS + k) * SLOT + row, PEERS, stride=2 * SLOT), :] = values[k * PEERS:k * PEERS + PEERS]
    for q in range(4):
        put(2 * CELLS + q, words[:PEERS, q * 128:q * 128 + 128])
        put_later(2 * CELLS + q, words[PEERS:, q * 128:q * 128 + 128])
    load.wait()

    def cells(chosen, store):
        blank = jnp.zeros((chosen.shape[0], 256 - CIN), f32)

        def some(i, carry):
            for u in range(3):
                c = i * 3 + u
                found = jnp.dot(chosen, rep[:, c].reshape(EP_DEV * EP_LEN, CIN), preferred_element_type=f32)
                store(c, found[:, :128])
                store(CELLS + c, jnp.concatenate([found[:, 128:], blank], axis=1))
            return carry
        lax.fori_loop(0, CELLS // 3, some, 0)
    cells(choose[:PEERS], put)

    def pack(p, carry):
        out[p] = stage[pl.ds(pl.multiple_of(p * SLOT, 8), SLOT), :].astype(bf16)
        return carry
    lax.fori_loop(0, PEERS, pack, 0)
    each(lambda d: frame(d).start())
    got[me] = out[me]
    cells(choose[PEERS:], put_later)

    def pack_later(p, carry):
        later_ref[p] = stage[pl.ds(pl.multiple_of((PEERS + p) * SLOT, 8), SLOT), :].astype(bf16)
        return carry
    lax.fori_loop(0, 2 * PEERS, pack_later, 0)
    each(lambda d: ask(d).wait_send())
    each(lambda d: frame(d).wait_recv())
    got_ref[...] = got[...]
    each(lambda d: frame(d).wait_send())


def fetch(owner, row, step, replay, instructions):
    V = pl.BlockSpec(memory_space=pltpu.VMEM)
    return pl.pallas_call(
        fetch_kernel,
        out_shape=(jax.ShapeDtypeStruct((PEERS, SLOT, 128), bf16), jax.ShapeDtypeStruct((2 * PEERS, SLOT, 128), bf16)),
        in_specs=[V, V, V, pl.BlockSpec(memory_space=pl.ANY), V], out_specs=(V, V),
        scratch_shapes=[pltpu.VMEM((EP_DEV, CELLS, EP_LEN, CIN), bf16), pltpu.VMEM((8, 128), jnp.int32), pltpu.VMEM((PEERS, 8, 128), jnp.int32),
                        pltpu.VMEM((PEERS * RANKS * SLOT, 128), f32), pltpu.VMEM((PEERS, SLOT, 128), bf16),
                        pltpu.VMEM((PEERS, SLOT, 128), bf16), pltpu.SemaphoreType.DMA,
                        pltpu.SemaphoreType.DMA((PEERS,)), pltpu.SemaphoreType.DMA((PEERS,)),
                        pltpu.SemaphoreType.DMA((PEERS,)), pltpu.SemaphoreType.DMA((PEERS,))],
        compiler_params=pltpu.CompilerParams(vmem_limit_bytes=56 * 2**20, collective_id=2, has_side_effects=True),
        name="fetch_frames",
    )(owner, row, step, replay.transpose(0, 2, 1, 3), instructions)


def vpu_block(pre, sc, dw_ref, F, S1, M, sec, prec, gk_ref):
    row = lambda c: slice(c * 8, c * 8 + 8)
    tap = lambda t: dw_ref[t * 8:t * 8 + 8, :]
    acc = [gk_ref[t * 8:t * 8 + 8, :] for t in range(9)]
    get = lambda ref, i: [ref[row(i * 9 + k), :] for k in range(9)] if 0 <= i < 9 else None

    def activate(i):
        for k in range(9):
            c = i * 9 + k
            h = pre[row(c), :]
            t = jnp.tanh(h)
            u = 1.0 + t
            F[row(c), :] = (h * u).astype(bf16).astype(f32)
            S1[row(c), :] = u * (1.0 + h * (1.0 - t))

    def ahead(i):
        rows3 = (get(F, i - 1), get(F, i), get(F, i + 1))
        for k in range(9):
            near = [(3 * r + c, rows3[r][k + c - 1]) for r in range(3) if rows3[r] for c in range(3) if 0 <= k + c - 1 < 9]
            h = None
            for t, v in near:
                h = tap(t) * v if h is None else h + tap(t) * v
            t = jnp.tanh(h)
            u = 1.0 + t
            sec[row(i * 9 + k), :] = h * u
            mc = sc[row(i * 9 + k), :] * (u * (1.0 + h * (1.0 - t)))
            M[row(i * 9 + k), :] = mc
            for t, v in near:
                acc[t] = acc[t] + mc * v

    def back(i):
        rows3 = (get(M, i + 1), get(M, i), get(M, i - 1))
        for k in range(9):
            total = None
            for r in range(3):
                for c in range(3):
                    if rows3[r] and 0 <= k - c + 1 < 9:
                        term = tap(3 * r + c) * rows3[r][k - c + 1]
                        total = term if total is None else total + term
            prec[row(i * 9 + k), :] = total * S1[row(i * 9 + k), :]
    for i in range(9):
        activate(i)
    for i in range(9):
        ahead(i)
    for i in range(9):
        back(i)
    for t in range(9):
        gk_ref[t * 8:t * 8 + 8, :] = acc[t]


def sort_frames(own_ref, named, rank, order):
    def clear(p, c):
        named[p] = 0
        return c
    lax.fori_loop(0, PEERS, clear, 0)

    def note(j, counts):
        o = own_ref[j]
        r = named[o]
        named[o] = r + 1
        rank[j] = r
        return (counts[0] + (r == 0).astype(jnp.int32), counts[1] + (r == 1).astype(jnp.int32))
    n0, n1 = lax.fori_loop(0, FR, note, (jnp.int32(0), jnp.int32(0)))

    def place_frame(j, at):
        r = rank[j]
        p = jnp.where(r == 0, at[0], jnp.where(r == 1, at[1], at[2]))
        order[p] = j
        return tuple(a + (r == k).astype(jnp.int32) for k, a in enumerate(at))
    lax.fori_loop(0, FR, place_frame, (jnp.int32(0), n0, n0 + n1))
    return n0


def prepare(wx_ref, kern_ref, wj_ref, we, dw, wp, wpt):
    we[...] = jnp.zeros_like(we)
    we[:CIN, :HID] = wx_ref[...] * jnp.asarray(0.5, bf16)
    wp[:HID, :] = wj_ref[...]
    wp[HID:, :] = jnp.zeros((HP - HID, COUT), bf16)
    wpt[...] = wp[...].T * jnp.asarray(0.5, bf16)
    taps = jnp.concatenate([kern_ref[...] * 0.5, jnp.zeros((9, HP - HID), f32)], axis=1)
    for k in range(NL):
        for t in range(9):
            dw[k, t * 8:t * 8 + 8, :] = jnp.broadcast_to(taps[t:t + 1, k * 128:k * 128 + 128], (8, 128))


def block_kernel(last, *refs):
    if last:
        (own_ref, got_ref, g_ref, fw_ref, more_ref, we_ref, dw_ref, wp_ref, wpt_ref, fc0, e0, ge0, gpt0, gk0, tok0,
         tok_ref, sum_ref, *scratch) = refs
        (named, rank, order, x32, xb, g32, pc, e32, pre, sc, sec, prec, secb, precb, proj, F, S1, M, tokens, tok_sem,
         ge, gpt, gk, fc, em, ge1, gpt1, gk1, sums_sem) = scratch
        loads = [pltpu.make_async_copy(src, dst, sums_sem.at[n]) for n, (src, dst) in enumerate(((ge0, ge1), (gpt0, gpt1), (gk0, gk1)))]
        for load in loads:
            load.start()
        fc[...] = fc0[...]
        em[...] = e0[...]
    else:
        (own_ref, got_ref, g_ref, fw_ref, wx_ref, kern_ref, wj_ref,
         we_ref, dw_ref, wp_ref, wpt_ref, fc, em, ge, gpt, gk, tok_ref, *scratch) = refs
        (named, rank, order, x32, xb, g32, pc, e32, pre, sc, sec, prec, secb, precb, proj, F, S1, M, tokens, tok_sem) = scratch
        prepare(wx_ref, kern_ref, wj_ref, we_ref, dw_ref, wp_ref, wpt_ref)
    for ref in (gk, ge, gpt):
        ref[...] = jnp.zeros_like(ref)
    early = sort_frames(own_ref, named, rank, order) // TILE
    first, stop = (early, NT) if last else (0, early)

    def tile(ft, carry):
        for f in range(TILE):
            p = ft * TILE + f
            keep = jnp.where(p < FR, 1.0, 0.0)
            j = order[jnp.minimum(p, FR - 1)]
            held = got_ref[own_ref[j]]
            if last:
                later = more_ref[own_ref[j] * 2 + jnp.maximum(rank[j], 1) - 1]
                held = jnp.where(rank[j] == 0, held, later)
            held = held.astype(f32) * keep
            for l in range(2):
                x32[l, pl.ds(f, CELLS, stride=TILE), :] = held[l * CELLS:l * CELLS + CELLS]
            for q in range(4):
                e32[f:f + 1, q * 128:q * 128 + 128] = held[2 * CELLS + q:2 * CELLS + q + 1]
            for l in range(3):
                g32[l, pl.ds(f, CELLS, stride=TILE), :] = g_ref[j, :, l * 128:l * 128 + 128].astype(f32) * keep
        for l in range(2):
            xb[:, l * 128:l * 128 + 128] = x32[l].astype(bf16)
        eb = e32[...].astype(bf16)
        em[ft] = eb
        fm = jnp.dot(eb, fw_ref[...], preferred_element_type=f32)
        scale, shift = 1.0 + fm[:, :COUT], fm[:, COUT:]
        for l in range(3):
            sl = slice(l * 128, l * 128 + 128)
            pc[:, sl] = (g32[l].reshape(CELLS, TILE, 128) * scale[None, :, sl]).reshape(ROWS, 128).astype(bf16)
        hidden = jnp.dot(xb[...], we_ref[...], preferred_element_type=f32)
        for k in range(NL):
            pre[k] = hidden[:, k * 128:k * 128 + 128]
        hidden = jnp.dot(pc[...], wpt_ref[...], preferred_element_type=f32)
        for k in range(NL):
            sc[k] = hidden[:, k * 128:k * 128 + 128]

        def one(k, n):
            vpu_block(pre.at[k], sc.at[k], dw_ref.at[k], F.at[n], S1.at[n], M.at[n], sec.at[k], prec.at[k], gk.at[k])

        def lanes(i, carry):
            one(2 * i, 0)
            one(2 * i + 1, 1)
            return carry
        lax.fori_loop(0, NL // 2, lanes, 0)
        one(NL - 1, 0)
        for k in range(NL):
            secb[:, k * 128:k * 128 + 128] = sec[k].astype(bf16)
            precb[:, k * 128:k * 128 + 128] = prec[k].astype(bf16)
        pj = jnp.dot(secb[...], wp_ref[...], preferred_element_type=f32)
        for l in range(3):
            sl = slice(l * 128, l * 128 + 128)
            g3, pj3 = g32[l].reshape(CELLS, TILE, 128), pj[:, sl].reshape(CELLS, TILE, 128)
            fc[ft, :, sl] = jnp.sum(g3 * pj3, axis=0)
            fc[ft, :, COUT + l * 128:COUT + l * 128 + 128] = jnp.sum(g3, axis=0)
            proj[l] = (pj3 * scale[None, :, sl] + shift[None, :, sl]).reshape(ROWS, 128)
        def token_copy(f):
            j = order[jnp.minimum(ft * TILE + f, FR - 1)]
            return pltpu.make_async_copy(tokens.at[f], tok_ref.at[j], tok_sem.at[f])
        for f in range(TILE):
            for l in range(3):
                tokens[f, :, l * 128:l * 128 + 128] = proj[l, pl.ds(f, CELLS, stride=TILE), :].astype(bf16)

            @pl.when(ft * TILE + f < FR)
            def _(f=f):
                token_copy(f).start()
        tn = (((0,), (0,)), ((), ()))
        ge[...] += lax.dot_general(xb[...], precb[...], tn, preferred_element_type=f32)
        gpt[...] += lax.dot_general(pc[...], secb[...], tn, preferred_element_type=f32)
        for f in range(TILE):
            @pl.when(ft * TILE + f < FR)
            def _(f=f):
                token_copy(f).wait()
        return carry
    lax.fori_loop(first, stop, tile, 0)
    if not last:
        return
    for load in loads:
        load.wait()
    for k in range(NL):
        ln = slice(k * 128, k * 128 + 128)
        sum_ref[GE + k * 240:GE + k * 240 + 240, :] = (ge[:240, ln] + ge1[:240, ln]).astype(bf16)
        taps = jnp.sum((gk[k] + gk1[k]).reshape(9, 8, 128), axis=1)
        sum_ref[GK + k * 16:GK + k * 16 + 16, :] = jnp.concatenate([taps, jnp.zeros((7, 128), f32)], axis=0).astype(bf16)
    for l in range(3):
        rows = slice(l * 128, l * 128 + 128)
        sum_ref[GP + l * HID:GP + l * HID + HID, :] = (gpt[rows, :] + gpt1[rows, :]).T[:HID].astype(bf16)
    words = em[...].astype(f32).reshape(NT * TILE, EMB).astype(bf16)
    cots = fc[...].reshape(NT * TILE, 2 * COUT).astype(bf16)
    gf = lax.dot_general(words, cots, (((0,), (0,)), ((), ())), preferred_element_type=f32).astype(bf16)
    for l in range(6):
        sum_ref[GF + l * EMB:GF + l * EMB + EMB, :] = gf[:, l * 128:l * 128 + 128]
    sum_ref[GF + 6 * EMB:, :] = jnp.zeros((GR - GF - 6 * EMB, 128), bf16)


def block(last, owner, arrays):
    V, A = pl.BlockSpec(memory_space=pltpu.VMEM), pl.BlockSpec(memory_space=pl.ANY)
    S = lambda *shape, t=f32: pltpu.VMEM(shape, t)
    I = lambda n: pltpu.SMEM((n,), jnp.int32)
    O = jax.ShapeDtypeStruct
    weights = [((256, HP), bf16), ((NL, 72, 128), f32), ((HP, COUT), bf16), ((COUT, HP), bf16)]
    frames = [((NT, TILE, 2 * COUT), f32), ((NT, TILE, EMB), bf16)]
    sums = [((256, HP), f32), ((COUT, HP), f32), ((NL, 72, 128), f32)]
    tok = O((FR, CELLS, COUT), bf16)
    scratch = [I(PEERS), I(FR), I(FR), S(2, ROWS, 128), S(ROWS, 256, t=bf16), S(3, ROWS, 128), S(ROWS, COUT, t=bf16), S(TILE, EMB),
               S(NL, ROWS, 128), S(NL, ROWS, 128), S(NL, ROWS, 128), S(NL, ROWS, 128), S(ROWS, HP, t=bf16), S(ROWS, HP, t=bf16),
               S(3, ROWS, 128), S(2, ROWS, 128), S(2, ROWS, 128), S(2, ROWS, 128), S(TILE, CELLS, COUT, t=bf16), pltpu.SemaphoreType.DMA((TILE,))]
    smem = pl.BlockSpec(memory_space=pltpu.SMEM)
    if last:
        out_shape, out_specs = (tok, O((GR, 128), bf16)), (A, V)
        in_specs = [smem] + [V] * 10 + [A] * 4
        scratch += [S(*shape, t=kind) for shape, kind in sums + frames + sums] + [pltpu.SemaphoreType.DMA((3,))]
        aliases = {14: 0}
    else:
        out_shape = tuple(O(*h) for h in weights + frames + sums) + (tok,)
        out_specs, in_specs, aliases = (V,) * 9 + (A,), [smem] + [V] * 6, {}
    return pl.pallas_call(
        functools.partial(block_kernel, last),
        out_shape=out_shape, in_specs=in_specs, out_specs=out_specs, scratch_shapes=scratch, input_output_aliases=aliases,
        compiler_params=pltpu.CompilerParams(vmem_limit_bytes=63 * 2**20),
        cost_estimate=pl.CostEstimate(flops=2 * 10**10, bytes_accessed=2 * 10**8, transcendentals=8 * 10**6),
        name="late_frames" if last else "early_frames",
    )(owner, *arrays)


PIECES = (32, 32, 16)
STARTS = (0, 4096, 8192)
ORDERS = (("x", "y", "z"), ("y", "z", "x"), ("z", "x", "y"))


def place():
    dp, rep = lax.axis_index("dp"), lax.axis_index("replica")
    return {"x": rep, "y": dp // 8, "z": (dp // 2) % 4, "core": dp % 2}


def device_of(at):
    return ((at["y"] * 4 + at["z"]) * 2 + at["core"], at["x"])


def shifted(at, axis, d):
    size = 2 if axis == "core" else 4
    other = dict(at)
    other[axis] = (at[axis] + d) % size
    return other


def reduce_kernel(g_ref, sum_ref, total, part, r0, r1, r2, r3, send, recv):
    at = place()
    barrier = pltpu.get_barrier_semaphore()
    peers = [shifted(at, "core", 1)] + [shifted(at, a, d) for a in "xyz" for d in (1, 2, 3)]
    for p in peers:
        pl.semaphore_signal(barrier, inc=1, device_id=device_of(p), device_id_type=pl.DeviceIdType.MESH)
    pl.semaphore_wait(barrier, len(peers))
    land = (r0, r1, r2, r3)
    waits = []

    def push(src, dst, stage, s, d, peer):
        copy = pltpu.make_async_remote_copy(src_ref=src, dst_ref=dst, send_sem=send.at[stage, s, d], recv_sem=recv.at[stage, s, d],
                                            device_id=device_of(peer), device_id_type=pl.DeviceIdType.MESH)
        copy.start()
        waits.append(copy)
        return copy

    def span(base, index, rows):
        return pl.ds(pl.multiple_of(base + index * rows, 16), rows)

    state = []
    for s, r in enumerate(PIECES):
        base, half = STARTS[s], 64 * r
        peer = shifted(at, "core", 1)
        c = push(g_ref.at[span(base, peer["core"], half)], r0.at[pl.ds(base // 2, half)], 0, s, 0, peer)
        state.append([c])
    for stage in (1, 2, 3):
        for s, r in enumerate(PIECES):
            axis = ORDERS[s][stage - 1]
            have = r * 4 ** (4 - stage)
            base = STARTS[s] // 2
            for c in state[s]:
                c.wait_recv()
            if stage == 1:
                mine = g_ref[span(STARTS[s], at["core"], have)].astype(f32) + r0[pl.ds(base, have)].astype(f32)
            else:
                prev = land[stage - 1]
                pb = base // 4 ** (stage - 1)
                old = part[stage - 2, span(base, at[ORDERS[s][stage - 2]], have)].astype(f32)
                mine = old
                for d in (1, 2, 3):
                    mine = mine + prev[d - 1, pl.ds(pb, have)].astype(f32)
            part[stage - 1, pl.ds(base, have)] = mine.astype(bf16)
            state[s] = []
            for d in (1, 2, 3):
                peer = shifted(at, axis, d)
                if stage == 3:
                    src, dst = part.at[2, pl.ds(base, have)], r3.at[d - 1, pl.ds(base // 16, have)]
                else:
                    block = have // 4
                    src = part.at[stage - 1, span(base, peer[axis], block)]
                    dst = land[stage].at[d - 1, pl.ds(base // 4 ** stage, block)]
                state[s].append(push(src, dst, stage, s, d - 1, peer))
    where = []
    for s, r in enumerate(PIECES):
        for c in state[s]:
            c.wait_recv()
        base, have = STARTS[s] // 2, 4 * r
        own = part[2, pl.ds(base, have)].astype(f32)
        near, far, back = [r3[d, pl.ds(base // 16, have)].astype(f32) for d in range(3)]
        a1, a2, a3 = ORDERS[s]
        where.append((at["core"] * 4 + at[a1]) * 4 + at[a2])
        total[span(STARTS[s], where[s], have)] = ((own + far) + (near + back)).astype(bf16)
        state[s] = []
    for stage in (5, 6, 7):
        for s, r in enumerate(PIECES):
            for c in state[s]:
                c.wait_recv()
            rows = r * 4 ** (stage - 4)
            index = where[s] // 4 ** (stage - 5)
            sl = span(STARTS[s], index, rows)
            state[s] = []
            if stage == 7:
                state[s].append(push(total.at[sl], total.at[sl], stage, s, 0, shifted(at, "core", 1)))
            else:
                axis = ORDERS[s][6 - stage]
                for d in (1, 2, 3):
                    state[s].append(push(total.at[sl], total.at[sl], stage, s, d - 1, shifted(at, axis, d)))
    for s in range(3):
        for c in state[s]:
            c.wait_recv()
    for c in waits:
        c.wait_send()
    sum_ref[...] = total[...]


def spread_kernel(total, ge_ref, gk_ref, gp_ref, gf_ref):
    for lt in range(11):
        w = min(128, HID - lt * 128)
        ge_ref[:, lt * 128:lt * 128 + w] = total[GE + lt * 240:GE + lt * 240 + 240].astype(f32)[:CIN, :w]
        gk_ref[:, lt * 128:lt * 128 + w] = total[GK + lt * 16:GK + lt * 16 + 16].astype(f32)[:9, :w]
    for l in range(3):
        gp_ref[:, l * 128:l * 128 + 128] = total[GP + l * HID:GP + l * HID + HID].astype(f32)
    for l in range(6):
        gf_ref[:, l * 128:l * 128 + 128] = total[GF + l * EMB:GF + l * EMB + EMB].astype(f32)


def all_reduce(g):
    V = pl.BlockSpec(memory_space=pltpu.VMEM)
    total = pl.pallas_call(
        reduce_kernel, out_shape=jax.ShapeDtypeStruct((GR, 128), bf16), in_specs=[V], out_specs=V,
        scratch_shapes=[pltpu.VMEM((GR, 128), bf16), pltpu.VMEM((3, GR // 2, 128), bf16), pltpu.VMEM((GR // 2, 128), bf16),
                        pltpu.VMEM((3, GR // 8, 128), bf16), pltpu.VMEM((3, GR // 32, 128), bf16), pltpu.VMEM((3, GR // 32, 128), bf16),
                        pltpu.SemaphoreType.DMA((8, 3, 3)), pltpu.SemaphoreType.DMA((8, 3, 3))],
        compiler_params=pltpu.CompilerParams(vmem_limit_bytes=32 * 2**20, collective_id=1, has_side_effects=True),
        name="grad_sum",
    )(g)
    return pl.pallas_call(
        spread_kernel,
        out_shape=(jax.ShapeDtypeStruct((CIN, HID), f32), jax.ShapeDtypeStruct((9, HID), f32),
                   jax.ShapeDtypeStruct((HID, COUT), f32), jax.ShapeDtypeStruct((EMB, 2 * COUT), f32)),
        in_specs=[V], out_specs=(V,) * 4, compiler_params=pltpu.CompilerParams(vmem_limit_bytes=32 * 2**20), name="grad_spread",
    )(total)


def per_device(replay, instructions, owners, episode_rows, frame_steps, w_expand, dw_kernel, w_project, film_weight, token_grad):
    owner = owners[:, 0]
    got, later = fetch(owner.reshape(1, FR), episode_rows.reshape(1, FR), frame_steps.reshape(1, FR), replay, instructions)
    more = lax.all_to_all(later.reshape(PEERS, 2, SLOT, 128), "dp", split_axis=0, concat_axis=0, tiled=True).reshape(2 * PEERS, SLOT, 128)
    g = token_grad.reshape(FR, CELLS, COUT)
    *weights, cots, words, grad_e, grad_p, grad_k, tokens = block(False, owner, (got, g, film_weight, w_expand, dw_kernel, w_project))
    tokens, partial_sums = block(True, owner, (got, g, film_weight, more, *weights, cots, words, grad_e, grad_p, grad_k, tokens))
    return (tokens.reshape(token_grad.shape), *all_reduce(partial_sums))


def solution(mesh):
    split = ("dp", "replica")
    in_specs = (P(split), P(split), P(split), P(split), P(split), P(), P(), P(), P(), P(split))
    return jax.shard_map(per_device, mesh=mesh, in_specs=in_specs, out_specs=(P(split), P(), P(), P(), P()), check_vma=False)
```

```python
import functools
import jax, jax.numpy as jnp
from jax import lax
from jax.experimental import pallas as pl
from jax.experimental.pallas import tpu as pltpu
from jax.sharding import PartitionSpec as P

SIDE, CELLS, TILE = 9, 81, 8
CIN, HID, COUT, EMB, FR = 232, 1392, 384, 512, 36
HP = 1408
NL = HP // 128
NT = 5
ROWS = CELLS * TILE
PEERS, RANKS, SLOT = 32, 3, 176
EP_DEV, EP_LEN = 8, 24
GR = 10240
GE, GK, GP, GF = 0, 2640, 2816, 6992
f32, bf16 = jnp.float32, jnp.bfloat16


def fetch_kernel(own_ref, row_ref, step_ref, rep_ref, ins_ref, got_ref, later_ref,
                 rep, ask_ref, asks, stage, out, got, rep_sem, ask_send, ask_recv, send, recv):
    me, rail = lax.axis_index("dp"), lax.axis_index("replica")
    load = pltpu.make_async_copy(rep_ref, rep, rep_sem)
    load.start()
    ask_ref[...] = jnp.full((8, 128), -1, jnp.int32)
    ask_ref[0:1, :FR] = own_ref[...]
    ask_ref[1:2, :FR] = row_ref[...] * EP_LEN + step_ref[...]
    barrier = pltpu.get_barrier_semaphore()

    def peer(d):
        return lax.rem(me + d, PEERS)

    def greet(d, c):
        pl.semaphore_signal(barrier, inc=1, device_id=(peer(d), rail), device_id_type=pl.DeviceIdType.MESH)
        return c
    lax.fori_loop(1, PEERS, greet, 0)
    pl.semaphore_wait(barrier, PEERS - 1)

    def ask(d):
        return pltpu.make_async_remote_copy(src_ref=ask_ref, dst_ref=asks.at[me], send_sem=ask_send.at[d], recv_sem=ask_recv.at[d],
                                            device_id=(peer(d), rail), device_id_type=pl.DeviceIdType.MESH)

    def frame(d):
        return pltpu.make_async_remote_copy(src_ref=out.at[peer(d)], dst_ref=got.at[me], send_sem=send.at[d], recv_sem=recv.at[d],
                                            device_id=(peer(d), rail), device_id_type=pl.DeviceIdType.MESH)

    def each(f):
        def body(d, c):
            f(d)
            return c
        lax.fori_loop(1, PEERS, body, 0)
    each(lambda d: ask(d).start())
    asks[me] = ask_ref[...]
    zero = jnp.zeros((PEERS * RANKS, 128), f32)
    for r in range(2 * CELLS + 4, SLOT):
        stage[pl.ds(r, PEERS * RANKS, stride=SLOT), :] = zero
    each(lambda d: ask(d).wait_recv())
    owner, wanted = asks[:, 0, :], asks[:, 1, :]
    mine = owner == me
    before = lax.broadcasted_iota(jnp.int32, (128, 128), 0) < lax.broadcasted_iota(jnp.int32, (128, 128), 1)
    rank = jnp.dot(jnp.where(mine, 1.0, 0.0).astype(bf16), jnp.where(before, 1.0, 0.0).astype(bf16), preferred_element_type=f32)
    wide = wanted.astype(f32)
    picks = []
    for k in range(RANKS):
        hit = mine & (rank > k - 0.5) & (rank < k + 0.5)
        picks.append(jnp.sum(jnp.where(hit, wide + 1.0, 0.0), axis=1, keepdims=True) - 1.0)
    pick = jnp.concatenate(picks, axis=0)
    at = lax.broadcasted_iota(jnp.int32, (PEERS * RANKS, EP_DEV * EP_LEN), 1).astype(f32)
    choose = jnp.where(pick == at, 1.0, 0.0).astype(bf16)
    low = lax.broadcasted_iota(jnp.int32, (PEERS * RANKS, EP_DEV), 1).astype(f32) * EP_LEN
    which = jnp.where((pick >= low) & (pick < low + EP_LEN), 1.0, 0.0).astype(bf16)
    words = jnp.dot(which, ins_ref[...], preferred_element_type=f32)

    def put(row, values):
        stage[pl.ds(row, PEERS, stride=SLOT), :] = values[:PEERS]

    def put_later(row, values):
        for k in range(2):
            stage[pl.ds((PEERS + k) * SLOT + row, PEERS, stride=2 * SLOT), :] = values[k * PEERS:k * PEERS + PEERS]
    for q in range(4):
        put(2 * CELLS + q, words[:PEERS, q * 128:q * 128 + 128])
        put_later(2 * CELLS + q, words[PEERS:, q * 128:q * 128 + 128])
    load.wait()

    def cells(chosen, store):
        blank = jnp.zeros((chosen.shape[0], 256 - CIN), f32)

        def some(i, carry):
            for u in range(3):
                c = i * 3 + u
                found = jnp.dot(chosen, rep[:, c].reshape(EP_DEV * EP_LEN, CIN), preferred_element_type=f32)
                store(c, found[:, :128])
                store(CELLS + c, jnp.concatenate([found[:, 128:], blank], axis=1))
            return carry
        lax.fori_loop(0, CELLS // 3, some, 0)
    cells(choose[:PEERS], put)

    def pack(p, carry):
        out[p] = stage[pl.ds(pl.multiple_of(p * SLOT, 8), SLOT), :].astype(bf16)
        return carry
    lax.fori_loop(0, PEERS, pack, 0)
    each(lambda d: frame(d).start())
    got[me] = out[me]
    cells(choose[PEERS:], put_later)

    def pack_later(p, carry):
        later_ref[p] = stage[pl.ds(pl.multiple_of((PEERS + p) * SLOT, 8), SLOT), :].astype(bf16)
        return carry
    lax.fori_loop(0, 2 * PEERS, pack_later, 0)
    each(lambda d: ask(d).wait_send())
    each(lambda d: frame(d).wait_recv())
    got_ref[...] = got[...]
    each(lambda d: frame(d).wait_send())


def fetch(owner, row, step, replay, instructions):
    V = pl.BlockSpec(memory_space=pltpu.VMEM)
    return pl.pallas_call(
        fetch_kernel,
        out_shape=(jax.ShapeDtypeStruct((PEERS, SLOT, 128), bf16), jax.ShapeDtypeStruct((2 * PEERS, SLOT, 128), bf16)),
        in_specs=[V, V, V, pl.BlockSpec(memory_space=pl.ANY), V], out_specs=(V, V),
        scratch_shapes=[pltpu.VMEM((EP_DEV, CELLS, EP_LEN, CIN), bf16), pltpu.VMEM((8, 128), jnp.int32), pltpu.VMEM((PEERS, 8, 128), jnp.int32),
                        pltpu.VMEM((PEERS * RANKS * SLOT, 128), f32), pltpu.VMEM((PEERS, SLOT, 128), bf16),
                        pltpu.VMEM((PEERS, SLOT, 128), bf16), pltpu.SemaphoreType.DMA,
                        pltpu.SemaphoreType.DMA((PEERS,)), pltpu.SemaphoreType.DMA((PEERS,)),
                        pltpu.SemaphoreType.DMA((PEERS,)), pltpu.SemaphoreType.DMA((PEERS,))],
        compiler_params=pltpu.CompilerParams(vmem_limit_bytes=56 * 2**20, collective_id=2, has_side_effects=True),
        name="fetch_frames",
    )(owner, row, step, replay.transpose(0, 2, 1, 3), instructions)


def vpu_block(pre, sc, dw_ref, F, S1, M, sec, prec, gk_ref):
    row = lambda c: slice(c * 8, c * 8 + 8)
    tap = lambda t: dw_ref[t * 8:t * 8 + 8, :]
    acc = [gk_ref[t * 8:t * 8 + 8, :] for t in range(9)]
    get = lambda ref, i: [ref[row(i * 9 + k), :] for k in range(9)] if 0 <= i < 9 else None

    def activate(i):
        for k in range(9):
            c = i * 9 + k
            h = pre[row(c), :]
            t = jnp.tanh(h)
            u = 1.0 + t
            F[row(c), :] = (h * u).astype(bf16).astype(f32)
            S1[row(c), :] = u * (1.0 + h * (1.0 - t))

    def ahead(i):
        rows3 = (get(F, i - 1), get(F, i), get(F, i + 1))
        for k in range(9):
            near = [(3 * r + c, rows3[r][k + c - 1]) for r in range(3) if rows3[r] for c in range(3) if 0 <= k + c - 1 < 9]
            h = None
            for t, v in near:
                h = tap(t) * v if h is None else h + tap(t) * v
            t = jnp.tanh(h)
            u = 1.0 + t
            sec[row(i * 9 + k), :] = h * u
            mc = sc[row(i * 9 + k), :] * (u * (1.0 + h * (1.0 - t)))
            M[row(i * 9 + k), :] = mc
            for t, v in near:
                acc[t] = acc[t] + mc * v

    def back(i):
        rows3 = (get(M, i + 1), get(M, i), get(M, i - 1))
        for k in range(9):
            total = None
            for r in range(3):
                for c in range(3):
                    if rows3[r] and 0 <= k - c + 1 < 9:
                        term = tap(3 * r + c) * rows3[r][k - c + 1]
                        total = term if total is None else total + term
            prec[row(i * 9 + k), :] = total * S1[row(i * 9 + k), :]
    for i in range(9):
        activate(i)
    for i in range(9):
        ahead(i)
    for i in range(9):
        back(i)
    for t in range(9):
        gk_ref[t * 8:t * 8 + 8, :] = acc[t]


def sort_frames(own_ref, named, rank, order):
    def clear(p, c):
        named[p] = 0
        return c
    lax.fori_loop(0, PEERS, clear, 0)

    def note(j, counts):
        o = own_ref[j]
        r = named[o]
        named[o] = r + 1
        rank[j] = r
        return (counts[0] + (r == 0).astype(jnp.int32), counts[1] + (r == 1).astype(jnp.int32))
    n0, n1 = lax.fori_loop(0, FR, note, (jnp.int32(0), jnp.int32(0)))

    def place_frame(j, at):
        r = rank[j]
        p = jnp.where(r == 0, at[0], jnp.where(r == 1, at[1], at[2]))
        order[p] = j
        return tuple(a + (r == k).astype(jnp.int32) for k, a in enumerate(at))
    lax.fori_loop(0, FR, place_frame, (jnp.int32(0), n0, n0 + n1))
    return n0


def prepare(wx_ref, kern_ref, wj_ref, we, dw, wp, wpt):
    we[...] = jnp.zeros_like(we)
    we[:CIN, :HID] = wx_ref[...] * jnp.asarray(0.5, bf16)
    wp[:HID, :] = wj_ref[...]
    wp[HID:, :] = jnp.zeros((HP - HID, COUT), bf16)
    wpt[...] = wp[...].T * jnp.asarray(0.5, bf16)
    taps = jnp.concatenate([kern_ref[...] * 0.5, jnp.zeros((9, HP - HID), f32)], axis=1)
    for k in range(NL):
        for t in range(9):
            dw[k, t * 8:t * 8 + 8, :] = jnp.broadcast_to(taps[t:t + 1, k * 128:k * 128 + 128], (8, 128))


def block_kernel(last, *refs):
    if last:
        (own_ref, got_ref, g_ref, fw_ref, more_ref, we_ref, dw_ref, wp_ref, wpt_ref, fc0, e0, ge0, gpt0, gk0, tok0,
         tok_ref, sum_ref, *scratch) = refs
        (named, rank, order, x32, xb, g32, pc, e32, pre, sc, sec, prec, secb, precb, proj, F, S1, M, tokens, tok_sem,
         ge, gpt, gk, fc, em, ge1, gpt1, gk1, sums_sem) = scratch
        loads = [pltpu.make_async_copy(src, dst, sums_sem.at[n]) for n, (src, dst) in enumerate(((ge0, ge1), (gpt0, gpt1), (gk0, gk1)))]
        for load in loads:
            load.start()
        fc[...] = fc0[...]
        em[...] = e0[...]
    else:
        (own_ref, got_ref, g_ref, fw_ref, wx_ref, kern_ref, wj_ref,
         we_ref, dw_ref, wp_ref, wpt_ref, fc, em, ge, gpt, gk, tok_ref, *scratch) = refs
        (named, rank, order, x32, xb, g32, pc, e32, pre, sc, sec, prec, secb, precb, proj, F, S1, M, tokens, tok_sem) = scratch
        prepare(wx_ref, kern_ref, wj_ref, we_ref, dw_ref, wp_ref, wpt_ref)
    for ref in (gk, ge, gpt):
        ref[...] = jnp.zeros_like(ref)
    early = sort_frames(own_ref, named, rank, order) // TILE
    first, stop = (early, NT) if last else (0, early)

    def tile(ft, carry):
        for f in range(TILE):
            p = ft * TILE + f
            keep = jnp.where(p < FR, 1.0, 0.0)
            j = order[jnp.minimum(p, FR - 1)]
            held = got_ref[own_ref[j]]
            if last:
                later = more_ref[own_ref[j] * 2 + jnp.maximum(rank[j], 1) - 1]
                held = jnp.where(rank[j] == 0, held, later)
            held = held.astype(f32) * keep
            for l in range(2):
                x32[l, pl.ds(f, CELLS, stride=TILE), :] = held[l * CELLS:l * CELLS + CELLS]
            for q in range(4):
                e32[f:f + 1, q * 128:q * 128 + 128] = held[2 * CELLS + q:2 * CELLS + q + 1]
            for l in range(3):
                g32[l, pl.ds(f, CELLS, stride=TILE), :] = g_ref[j, :, l * 128:l * 128 + 128].astype(f32) * keep
        for l in range(2):
            xb[:, l * 128:l * 128 + 128] = x32[l].astype(bf16)
        eb = e32[...].astype(bf16)
        em[ft] = eb
        fm = jnp.dot(eb, fw_ref[...], preferred_element_type=f32)
        scale, shift = 1.0 + fm[:, :COUT], fm[:, COUT:]
        for l in range(3):
            sl = slice(l * 128, l * 128 + 128)
            pc[:, sl] = (g32[l].reshape(CELLS, TILE, 128) * scale[None, :, sl]).reshape(ROWS, 128).astype(bf16)
        hidden = jnp.dot(xb[...], we_ref[...], preferred_element_type=f32)
        for k in range(NL):
            pre[k] = hidden[:, k * 128:k * 128 + 128]
        hidden = jnp.dot(pc[...], wpt_ref[...], preferred_element_type=f32)
        for k in range(NL):
            sc[k] = hidden[:, k * 128:k * 128 + 128]

        def one(k, n):
            vpu_block(pre.at[k], sc.at[k], dw_ref.at[k], F.at[n], S1.at[n], M.at[n], sec.at[k], prec.at[k], gk.at[k])

        def lanes(i, carry):
            one(2 * i, 0)
            one(2 * i + 1, 1)
            return carry
        lax.fori_loop(0, NL // 2, lanes, 0)
        one(NL - 1, 0)
        for k in range(NL):
            secb[:, k * 128:k * 128 + 128] = sec[k].astype(bf16)
            precb[:, k * 128:k * 128 + 128] = prec[k].astype(bf16)
        pj = jnp.dot(secb[...], wp_ref[...], preferred_element_type=f32)
        for l in range(3):
            sl = slice(l * 128, l * 128 + 128)
            g3, pj3 = g32[l].reshape(CELLS, TILE, 128), pj[:, sl].reshape(CELLS, TILE, 128)
            fc[ft, :, sl] = jnp.sum(g3 * pj3, axis=0)
            fc[ft, :, COUT + l * 128:COUT + l * 128 + 128] = jnp.sum(g3, axis=0)
            proj[l] = (pj3 * scale[None, :, sl] + shift[None, :, sl]).reshape(ROWS, 128)
        def token_copy(f):
            j = order[jnp.minimum(ft * TILE + f, FR - 1)]
            return pltpu.make_async_copy(tokens.at[f], tok_ref.at[j], tok_sem.at[f])
        for f in range(TILE):
            for l in range(3):
                tokens[f, :, l * 128:l * 128 + 128] = proj[l, pl.ds(f, CELLS, stride=TILE), :].astype(bf16)

            @pl.when(ft * TILE + f < FR)
            def _(f=f):
                token_copy(f).start()
        tn = (((0,), (0,)), ((), ()))
        ge[...] += lax.dot_general(xb[...], precb[...], tn, preferred_element_type=f32)
        gpt[...] += lax.dot_general(pc[...], secb[...], tn, preferred_element_type=f32)
        for f in range(TILE):
            @pl.when(ft * TILE + f < FR)
            def _(f=f):
                token_copy(f).wait()
        return carry
    lax.fori_loop(first, stop, tile, 0)
    if not last:
        return
    for load in loads:
        load.wait()
    for k in range(NL):
        ln = slice(k * 128, k * 128 + 128)
        sum_ref[GE + k * 240:GE + k * 240 + 240, :] = (ge[:240, ln] + ge1[:240, ln]).astype(bf16)
        taps = jnp.sum((gk[k] + gk1[k]).reshape(9, 8, 128), axis=1)
        sum_ref[GK + k * 16:GK + k * 16 + 16, :] = jnp.concatenate([taps, jnp.zeros((7, 128), f32)], axis=0).astype(bf16)
    for l in range(3):
        rows = slice(l * 128, l * 128 + 128)
        sum_ref[GP + l * HID:GP + l * HID + HID, :] = (gpt[rows, :] + gpt1[rows, :]).T[:HID].astype(bf16)
    words = em[...].astype(f32).reshape(NT * TILE, EMB).astype(bf16)
    cots = fc[...].reshape(NT * TILE, 2 * COUT).astype(bf16)
    gf = lax.dot_general(words, cots, (((0,), (0,)), ((), ())), preferred_element_type=f32).astype(bf16)
    for l in range(6):
        sum_ref[GF + l * EMB:GF + l * EMB + EMB, :] = gf[:, l * 128:l * 128 + 128]
    sum_ref[GF + 6 * EMB:, :] = jnp.zeros((GR - GF - 6 * EMB, 128), bf16)


def block(last, owner, arrays):
    V, A = pl.BlockSpec(memory_space=pltpu.VMEM), pl.BlockSpec(memory_space=pl.ANY)
    S = lambda *shape, t=f32: pltpu.VMEM(shape, t)
    I = lambda n: pltpu.SMEM((n,), jnp.int32)
    O = jax.ShapeDtypeStruct
    weights = [((256, HP), bf16), ((NL, 72, 128), f32), ((HP, COUT), bf16), ((COUT, HP), bf16)]
    frames = [((NT, TILE, 2 * COUT), f32), ((NT, TILE, EMB), bf16)]
    sums = [((256, HP), f32), ((COUT, HP), f32), ((NL, 72, 128), f32)]
    tok = O((FR, CELLS, COUT), bf16)
    scratch = [I(PEERS), I(FR), I(FR), S(2, ROWS, 128), S(ROWS, 256, t=bf16), S(3, ROWS, 128), S(ROWS, COUT, t=bf16), S(TILE, EMB),
               S(NL, ROWS, 128), S(NL, ROWS, 128), S(NL, ROWS, 128), S(NL, ROWS, 128), S(ROWS, HP, t=bf16), S(ROWS, HP, t=bf16),
               S(3, ROWS, 128), S(2, ROWS, 128), S(2, ROWS, 128), S(2, ROWS, 128), S(TILE, CELLS, COUT, t=bf16), pltpu.SemaphoreType.DMA((TILE,))]
    smem = pl.BlockSpec(memory_space=pltpu.SMEM)
    if last:
        out_shape, out_specs = (tok, O((GR, 128), bf16)), (A, V)
        in_specs = [smem] + [V] * 10 + [A] * 4
        scratch += [S(*shape, t=kind) for shape, kind in sums + frames + sums] + [pltpu.SemaphoreType.DMA((3,))]
        aliases = {14: 0}
    else:
        out_shape = tuple(O(*h) for h in weights + frames + sums) + (tok,)
        out_specs, in_specs, aliases = (V,) * 9 + (A,), [smem] + [V] * 6, {}
    return pl.pallas_call(
        functools.partial(block_kernel, last),
        out_shape=out_shape, in_specs=in_specs, out_specs=out_specs, scratch_shapes=scratch, input_output_aliases=aliases,
        compiler_params=pltpu.CompilerParams(vmem_limit_bytes=46 * 2**20),
        cost_estimate=pl.CostEstimate(flops=2 * 10**10, bytes_accessed=2 * 10**8, transcendentals=8 * 10**6),
        name="late_frames" if last else "early_frames",
    )(owner, *arrays)


PIECES = (32, 32, 16)
STARTS = (0, 4096, 8192)
ORDERS = (("x", "y", "z"), ("y", "z", "x"), ("z", "x", "y"))


def place():
    dp, rep = lax.axis_index("dp"), lax.axis_index("replica")
    return {"x": rep, "y": dp // 8, "z": (dp // 2) % 4, "core": dp % 2}


def device_of(at):
    return ((at["y"] * 4 + at["z"]) * 2 + at["core"], at["x"])


def shifted(at, axis, d):
    size = 2 if axis == "core" else 4
    other = dict(at)
    other[axis] = (at[axis] + d) % size
    return other


def reduce_kernel(g_ref, sum_ref, total, part, r0, r1, r2, r3, send, recv):
    at = place()
    barrier = pltpu.get_barrier_semaphore()
    peers = [shifted(at, "core", 1)] + [shifted(at, a, d) for a in "xyz" for d in (1, 2, 3)]
    for p in peers:
        pl.semaphore_signal(barrier, inc=1, device_id=device_of(p), device_id_type=pl.DeviceIdType.MESH)
    pl.semaphore_wait(barrier, len(peers))
    land = (r0, r1, r2, r3)
    waits = []

    def push(src, dst, stage, s, d, peer):
        copy = pltpu.make_async_remote_copy(src_ref=src, dst_ref=dst, send_sem=send.at[stage, s, d], recv_sem=recv.at[stage, s, d],
                                            device_id=device_of(peer), device_id_type=pl.DeviceIdType.MESH)
        copy.start()
        waits.append(copy)
        return copy

    def span(base, index, rows):
        return pl.ds(pl.multiple_of(base + index * rows, 16), rows)

    state = []
    for s, r in enumerate(PIECES):
        base, half = STARTS[s], 64 * r
        peer = shifted(at, "core", 1)
        c = push(g_ref.at[span(base, peer["core"], half)], r0.at[pl.ds(base // 2, half)], 0, s, 0, peer)
        state.append([c])
    for stage in (1, 2, 3):
        for s, r in enumerate(PIECES):
            axis = ORDERS[s][stage - 1]
            have = r * 4 ** (4 - stage)
            base = STARTS[s] // 2
            for c in state[s]:
                c.wait_recv()
            if stage == 1:
                mine = g_ref[span(STARTS[s], at["core"], have)].astype(f32) + r0[pl.ds(base, have)].astype(f32)
            else:
                prev = land[stage - 1]
                pb = base // 4 ** (stage - 1)
                old = part[stage - 2, span(base, at[ORDERS[s][stage - 2]], have)].astype(f32)
                mine = old
                for d in (1, 2, 3):
                    mine = mine + prev[d - 1, pl.ds(pb, have)].astype(f32)
            part[stage - 1, pl.ds(base, have)] = mine.astype(bf16)
            state[s] = []
            for d in (1, 2, 3):
                peer = shifted(at, axis, d)
                if stage == 3:
                    src, dst = part.at[2, pl.ds(base, have)], r3.at[d - 1, pl.ds(base // 16, have)]
                else:
                    block = have // 4
                    src = part.at[stage - 1, span(base, peer[axis], block)]
                    dst = land[stage].at[d - 1, pl.ds(base // 4 ** stage, block)]
                state[s].append(push(src, dst, stage, s, d - 1, peer))
    where = []
    for s, r in enumerate(PIECES):
        for c in state[s]:
            c.wait_recv()
        base, have = STARTS[s] // 2, 4 * r
        own = part[2, pl.ds(base, have)].astype(f32)
        near, far, back = [r3[d, pl.ds(base // 16, have)].astype(f32) for d in range(3)]
        a1, a2, a3 = ORDERS[s]
        where.append((at["core"] * 4 + at[a1]) * 4 + at[a2])
        total[span(STARTS[s], where[s], have)] = ((own + far) + (near + back)).astype(bf16)
        state[s] = []
    for stage in (5, 6, 7):
        for s, r in enumerate(PIECES):
            for c in state[s]:
                c.wait_recv()
            rows = r * 4 ** (stage - 4)
            index = where[s] // 4 ** (stage - 5)
            sl = span(STARTS[s], index, rows)
            state[s] = []
            if stage == 7:
                state[s].append(push(total.at[sl], total.at[sl], stage, s, 0, shifted(at, "core", 1)))
            else:
                axis = ORDERS[s][6 - stage]
                for d in (1, 2, 3):
                    state[s].append(push(total.at[sl], total.at[sl], stage, s, d - 1, shifted(at, axis, d)))
    for s in range(3):
        for c in state[s]:
            c.wait_recv()
    for c in waits:
        c.wait_send()
    sum_ref[...] = total[...]


def spread_kernel(total, ge_ref, gk_ref, gp_ref, gf_ref):
    for lt in range(11):
        w = min(128, HID - lt * 128)
        ge_ref[:, lt * 128:lt * 128 + w] = total[GE + lt * 240:GE + lt * 240 + 240].astype(f32)[:CIN, :w]
        gk_ref[:, lt * 128:lt * 128 + w] = total[GK + lt * 16:GK + lt * 16 + 16].astype(f32)[:9, :w]
    for l in range(3):
        gp_ref[:, l * 128:l * 128 + 128] = total[GP + l * HID:GP + l * HID + HID].astype(f32)
    for l in range(6):
        gf_ref[:, l * 128:l * 128 + 128] = total[GF + l * EMB:GF + l * EMB + EMB].astype(f32)


def all_reduce(g):
    V = pl.BlockSpec(memory_space=pltpu.VMEM)
    total = pl.pallas_call(
        reduce_kernel, out_shape=jax.ShapeDtypeStruct((GR, 128), bf16), in_specs=[V], out_specs=V,
        scratch_shapes=[pltpu.VMEM((GR, 128), bf16), pltpu.VMEM((3, GR // 2, 128), bf16), pltpu.VMEM((GR // 2, 128), bf16),
                        pltpu.VMEM((3, GR // 8, 128), bf16), pltpu.VMEM((3, GR // 32, 128), bf16), pltpu.VMEM((3, GR // 32, 128), bf16),
                        pltpu.SemaphoreType.DMA((8, 3, 3)), pltpu.SemaphoreType.DMA((8, 3, 3))],
        compiler_params=pltpu.CompilerParams(vmem_limit_bytes=32 * 2**20, collective_id=1, has_side_effects=True),
        name="grad_sum",
    )(g)
    return pl.pallas_call(
        spread_kernel,
        out_shape=(jax.ShapeDtypeStruct((CIN, HID), f32), jax.ShapeDtypeStruct((9, HID), f32),
                   jax.ShapeDtypeStruct((HID, COUT), f32), jax.ShapeDtypeStruct((EMB, 2 * COUT), f32)),
        in_specs=[V], out_specs=(V,) * 4, compiler_params=pltpu.CompilerParams(vmem_limit_bytes=32 * 2**20), name="grad_spread",
    )(total)


def per_device(replay, instructions, owners, episode_rows, frame_steps, w_expand, dw_kernel, w_project, film_weight, token_grad):
    owner = owners[:, 0]
    got, later = fetch(owner.reshape(1, FR), episode_rows.reshape(1, FR), frame_steps.reshape(1, FR), replay, instructions)
    more = lax.all_to_all(later.reshape(PEERS, 2, SLOT, 128), "dp", split_axis=0, concat_axis=0, tiled=True).reshape(2 * PEERS, SLOT, 128)
    g = token_grad.reshape(FR, CELLS, COUT)
    *weights, cots, words, grad_e, grad_p, grad_k, tokens = block(False, owner, (got, g, film_weight, w_expand, dw_kernel, w_project))
    tokens, partial_sums = block(True, owner, (got, g, film_weight, more, *weights, cots, words, grad_e, grad_p, grad_k, tokens))
    return (tokens.reshape(token_grad.shape), *all_reduce(partial_sums))


def solution(mesh):
    split = ("dp", "replica")
    in_specs = (P(split), P(split), P(split), P(split), P(split), P(), P(), P(), P(), P(split))
    return jax.shard_map(per_device, mesh=mesh, in_specs=in_specs, out_specs=(P(split), P(), P(), P(), P()), check_vma=False)
```
